256 devices in a mesh: ctx: 8 (over y, core), grp: 16 (over x_hi, z), tp: 2 (over x_lo).
Axes of the slice: x: 4 (x_hi: 2, x_lo: 2; x = x_hi * 2 + x_lo), y: 4, z: 8, core: 2. Of those that a mesh axis runs over, the one named last changes fastest.
Arguments:
- queries: bfloat16 [32, 1024, 4096], P(('grp', 'tp'), 'ctx'), may hold values from -32 to 32
- keys: bfloat16 [32, 1024, 1024], P(('grp', 'tp'), 'ctx'), may hold values from -6 to 6
- values: bfloat16 [32, 1024, 1024], P(('grp', 'tp'), 'ctx'), may hold values from -6 to 6
- documents: int32 [32, 1024], P(('grp', 'tp'), 'ctx'), may hold values from 0 to 7, never falling along the last dimension, each value on 1 to 512 neighbouring positions
- residual: bfloat16 [32, 1024, 4096], P(('grp', 'tp'), 'ctx'), may hold values from -6 to 6
- labels: int32 [32, 64], P(('grp', 'tp'), 'ctx'), may hold values from 0 to 127
- out_weight: bfloat16 [4096, 4096], P('ctx', ('grp', 'tp')), may hold values from -0.09375 to 0.09375
- norm_gain: bfloat16 [4096], P(('grp', 'tp')), may hold values from 0.25 to 1.75
- gate_weight: bfloat16 [4096, 14336], P('ctx', ('grp', 'tp')), may hold values from -0.09375 to 0.09375
- up_weight: bfloat16 [4096, 14336], P('ctx', ('grp', 'tp')), may hold values from -0.09375 to 0.09375
- down_weight: bfloat16 [14336, 4096], P(('grp', 'tp'), 'ctx'), may hold values from -0.046875 to 0.046875
- reward_weight: bfloat16 [4096], P(('grp', 'tp')), may hold values from -0.09375 to 0.09375
Outputs:
- attended: bfloat16 [32, 1024, 4096], P(('grp', 'tp'), 'ctx')
- labeled: bfloat16 [2048, 4096], P('ctx', ('grp', 'tp'))
- reward: float32 [2048], P('ctx')
The draws below stay inside these ranges and needn't reach their ends.
All inputs are finite; a program needn't handle non-finite values.
Results may differ from the reference program's by a relative error of at most 0.006.
Values may be sent and summed in bfloat16 or wider, within the bound.
A program may use at most 128 MiB of HBM per device.

```python
import math
import jax
import jax.numpy as jnp
import numpy as np
from jax import lax

D = 4096
H = 32
KVH = 8
HD = 128
FF = 14336
TOK_DEV = 128
LAB = 8
SEQS = 32
SEQ = 1024
ROWS = 2048
N_CTX = 8


def key_base(key):
    return jnp.clip(jax.random.normal(key, (SEQS, SEQ, KVH * HD), jnp.float32), -6.0, 6.0)


def draw_keys(key, part):
    base = key_base(key)
    return base.astype(jnp.bfloat16)


def draw_queries(key, part):
    key = jax.random.fold_in(key, 12)
    values_out = jax.random.normal(key, (SEQS, SEQ, D), jnp.float32)
    return jnp.clip(values_out, -32.0, 32.0).astype(jnp.bfloat16)


def with_ends(entries, key, smallest, high):
    longest = entries.shape.index(max(entries.shape))
    spots = []
    for shift in (0, 1):
        where = [jax.random.randint(jax.random.fold_in(key, axis), (), 0, length) for axis, length in enumerate(entries.shape)]
        where[longest] = (where[longest] + shift) % entries.shape[longest]
        spots.append(tuple(where))
    return entries.at[spots[0]].set(smallest).at[spots[1]].set(high)


def level_of(stream_key, extent, cuts, low, high):
    def one(position, blocks):
        steps = jax.random.uniform(jax.random.fold_in(jax.random.fold_in(stream_key, 6), position), (blocks,), jnp.float32, low / len(cuts), high / len(cuts))
        return jnp.repeat(jnp.exp(steps), extent[position] // blocks).reshape((-1,) + (1,) * (len(extent) - position - 1))

    factor_of = one(*cuts[0])
    for cut in cuts[1:]:
        factor_of = factor_of * one(*cut)
    return factor_of


def split_up(count, total, most, slope):
    loads = [(1 << 20) // math.isqrt(standing ** slope) + 1 for standing in range(2, count + 1)]
    spare, holding = total - most - (count - 1), [1] * (count - 1)
    while spare > 0:
        movable = [i for i in range(count - 1) if holding[i] < most]
        pool, budget = sum([loads[i] for i in movable]), spare
        for i in movable:
            extra = min(most - holding[i], max(1, budget * loads[i] // pool), spare)
            holding[i] = holding[i] + extra
            spare = spare - extra
    return np.array([most] + holding)


def ragged_sizes(stream_key, count, total, most, skew):
    if count == 2:
        one = jax.random.randint(stream_key, (), max(1, total - most), min(most, total - 1) + 1)
        return jnp.stack([one, total - one])
    lengths = jnp.asarray(split_up(count, total, most, skew), jnp.int32)
    pairs = (count - 1) // 2
    donor, sink = lengths[1:1 + 2 * pairs:2], lengths[2:2 + 2 * pairs:2]
    room = jnp.minimum(donor - 1, most - sink)
    moved = jax.random.randint(jax.random.fold_in(stream_key, 1), (pairs,), 0, 1 << 20) % (room + 1)
    lengths = lengths.at[1:1 + 2 * pairs:2].set(donor - moved).at[2:2 + 2 * pairs:2].set(sink + moved)
    return lengths[jax.random.permutation(jax.random.fold_in(stream_key, 2), count)]


def scatter_about(rng, dims, width, most, pieces=(), kind=jnp.bfloat16):
    values = width * jax.random.normal(rng, dims, jnp.float32)
    if pieces:
        values = values * level_of(rng, dims, pieces, -0.22, 0.18)
    return jnp.clip(values, -most, most).astype(kind)


def setup_inputs(seed: int = 0) -> dict:
    seeds = jax.random.split(jax.random.key(seed), 13)
    queries = draw_queries(jax.random.fold_in(seeds[12], 71), 0)
    keys = draw_keys(jax.random.fold_in(seeds[12], 71), 0)
    values = scatter_about(seeds[2], (SEQS, SEQ, KVH * HD), 1.0, 6.0, ((0, 32), (1, 8)))
    documents = jax.vmap(lambda own: jnp.searchsorted(jnp.cumsum(ragged_sizes(own, N_CTX, SEQ, SEQ // 2, 0)), jnp.arange(SEQ), side="right"))(jax.random.split(seeds[3], SEQS)).reshape((SEQS, SEQ)).astype(jnp.int32)
    residual = scatter_about(seeds[4], (SEQS, SEQ, D), 1.0, 6.0, ((0, 32), (1, 8)))
    labels = with_ends(jax.random.randint(seeds[5], (SEQS, N_CTX * LAB), 0, TOK_DEV), jax.random.fold_in(seeds[5], 1), 0, TOK_DEV - 1).astype(jnp.int32)
    out_weight = scatter_about(seeds[6], (D, D), D ** -0.5, 0.09375, ((0, 8), (1, 32)))
    norm_gain = jnp.clip(1.0 + 0.15 * jax.random.normal(seeds[7], (D,), jnp.float32), 0.25, 1.75).astype(jnp.bfloat16)
    gate_weight = scatter_about(seeds[8], (D, FF), D ** -0.5, 0.09375, ((0, 8), (1, 32)))
    up_weight = scatter_about(seeds[9], (D, FF), D ** -0.5, 0.09375, ((0, 8), (1, 32)))
    down_weight = scatter_about(seeds[10], (FF, D), FF ** -0.5, 0.046875, ((0, 32), (1, 8)))
    reward_weight = scatter_about(seeds[11], (D,), D ** -0.5, 0.09375, ((0, 32),))
    return dict(queries=queries, keys=keys, values=values, documents=documents, residual=residual, labels=labels, out_weight=out_weight, norm_gain=norm_gain, gate_weight=gate_weight, up_weight=up_weight, down_weight=down_weight, reward_weight=reward_weight)


def attend_block(query_rows, query_pos, query_doc, key_rows, value_rows, key_doc):
    count = query_rows.shape[0]
    group = H // KVH
    qf = query_rows.astype(jnp.float32).reshape(count, KVH, group, HD)
    kf = key_rows.astype(jnp.float32).reshape(key_rows.shape[0], KVH, HD)
    vf = value_rows.astype(jnp.float32).reshape(value_rows.shape[0], KVH, HD)
    key_pos = jnp.arange(key_rows.shape[0], dtype=jnp.int32)
    score = jnp.einsum('rkgd,skd->kgrs', qf, kf) * HD ** (-0.5)
    keep = (key_pos[None, :] <= query_pos[:, None]) & (key_doc[None, :] == query_doc[:, None])
    score = jnp.where(keep, score, -1e+30)
    top = lax.optimization_barrier(jnp.max(score, axis=-1, keepdims=True))
    weight = jnp.where(keep, jnp.exp(score - top), 0.0)
    total = lax.optimization_barrier(jnp.sum(weight, axis=-1))
    rounded = weight.astype(jnp.bfloat16).astype(jnp.float32)
    summed = jnp.einsum('kgrs,skd->kgrd', rounded, vf) / total[..., None]
    return jnp.transpose(summed, (2, 0, 1, 3)).reshape(count, D).astype(jnp.bfloat16)

def attend_trace(inputs):
    query_all, key_all, value_all, doc_all = inputs
    blocks = SEQ // TOK_DEV

    def one_block(index):
        start = (index * TOK_DEV).astype(jnp.int32)
        query_rows = lax.dynamic_slice_in_dim(query_all, start, TOK_DEV, 0)
        query_doc = lax.dynamic_slice_in_dim(doc_all, start, TOK_DEV, 0)
        query_pos = start + jnp.arange(TOK_DEV, dtype=jnp.int32)
        return attend_block(query_rows, query_pos, query_doc, key_all, value_all, doc_all)
    out = lax.map(one_block, jnp.arange(blocks, dtype=jnp.int32))
    return out.reshape(SEQ, D)

def reference(queries, keys, values, documents, residual, labels, out_weight, norm_gain, gate_weight, up_weight, down_weight, reward_weight):
    attended = lax.map(attend_trace, (queries, keys, values, documents))
    lab = labels.reshape(SEQS, N_CTX, LAB)
    pos = lab + (jnp.arange(N_CTX, dtype=jnp.int32) * TOK_DEV)[None, :, None]
    pos = jnp.transpose(pos, (1, 0, 2))
    trace = jnp.broadcast_to(jnp.arange(SEQS, dtype=jnp.int32)[None, :, None], pos.shape)
    picked = attended[trace, pos].reshape(ROWS, D)
    base = residual[trace, pos].reshape(ROWS, D)
    state = base.astype(jnp.float32) + jnp.dot(picked, out_weight, preferred_element_type=jnp.float32)
    mean_square = lax.optimization_barrier(jnp.mean(state * state, axis=-1, keepdims=True))
    normed = (state * lax.rsqrt(mean_square + 1e-05) * norm_gain.astype(jnp.float32)).astype(jnp.bfloat16)
    gate = jnp.dot(normed, gate_weight, preferred_element_type=jnp.float32)
    up = jnp.dot(normed, up_weight, preferred_element_type=jnp.float32)
    hidden = (jax.nn.silu(gate) * up).astype(jnp.bfloat16)
    labeled = (state + jnp.dot(hidden, down_weight, preferred_element_type=jnp.float32)).astype(jnp.bfloat16)
    reward = jnp.dot(labeled, reward_weight, preferred_element_type=jnp.float32)
    return (attended, labeled, reward)
```

```python
import functools
import math

import jax
import jax.numpy as jnp
from jax import lax
from jax.experimental import pallas as pl
from jax.experimental.pallas import tpu as pltpu
from jax.sharding import PartitionSpec as P

MESH = pl.DeviceIdType.MESH
NX, NY, NZ = 4, 4, 8
D, H, KVH, HD, FF = 4096, 32, 8, 128, 14336
TOK, LAB = 128, 8
ROWS = 256
FFL = 448
F32, BF16 = jnp.float32, jnp.bfloat16
SCALE2 = HD**-0.5 * math.log2(math.e)
NSEM = 176


def block_of(col):
    grp, tp = col // 2, col % 2
    return (grp // NZ) * 2 + tp, grp % NZ


def nt(a, b):
    return lax.dot_general(a, b, (((1,), (1,)), ((), ())), preferred_element_type=F32)


def body(
    q_ref,
    k_ref,
    v_ref,
    doc_ref,
    res_ref,
    lab_ref,
    ow_ref,
    gain_ref,
    gate_ref,
    up_ref,
    dn_ref,
    rw_ref,
    att_ref,
    labeled_ref,
    reward_ref,
    kbuf,
    vbuf,
    dbuf,
    ow,
    gu,
    dn,
    bias,
    qlab,
    plab,
    a0,
    a1,
    bsrc,
    bz,
    bx,
    state,
    s0,
    s1,
    acc,
    tb0,
    rx0,
    sb0,
    rz0,
    tb1,
    rp,
    rm,
    sp,
    sm,
    sb1,
    rx1,
    prx,
    prz,
    ss,
    rs,
    ls,
):
    ctx, grp, tp = lax.axis_index("ctx"), lax.axis_index("grp"), lax.axis_index("tp")
    y, core = ctx // 2, ctx % 2
    x, z = (grp // NZ) * 2 + tp, grp % NZ
    other = y * 2 + 1 - core

    def wrap(v, n):
        return lax.rem(v + n, n)

    def dev(axis, k):
        if axis == "y":
            return {"ctx": wrap(y + k, NY) * 2 + core}
        if axis == "core":
            return {"ctx": other}
        if axis == "z":
            return {"grp": (x // 2) * NZ + wrap(z + k, NZ)}
        there = wrap(x + k, NX)
        return {"grp": (there // 2) * NZ + z, "tp": there % 2}

    ids = iter(range(NSEM))
    sent = []

    def send(src, dst, axis, k, cond=None):
        i = next(ids)
        copy = pltpu.make_async_remote_copy(
            src_ref=src,
            dst_ref=dst,
            send_sem=ss.at[i],
            recv_sem=rs.at[i],
            device_id=dev(axis, k),
            device_id_type=MESH,
        )
        if cond is None:
            copy.start()
        else:
            pl.when(cond)(copy.start)
        sent.append((copy, cond))
        return i

    def recv(dst, i):
        pltpu.make_async_remote_copy(
            src_ref=dst,
            dst_ref=dst,
            send_sem=ss.at[i],
            recv_sem=rs.at[i],
            device_id={"ctx": other},
            device_id_type=MESH,
        ).wait_recv()

    barrier = pltpu.get_barrier_semaphore()
    partners = [("core", 1)]
    partners += [("y", k) for k in range(1, NY)]
    partners += [("x", k) for k in range(1, NX)]
    partners += [("z", k) for k in range(1, NZ)]
    for axis, k in partners:
        pl.semaphore_signal(barrier, inc=1, device_id=dev(axis, k), device_id_type=MESH)

    local = [
        pltpu.make_async_copy(k_ref.at[0], kbuf.at[ctx], ls.at[0]),
        pltpu.make_async_copy(v_ref.at[0], vbuf.at[ctx], ls.at[1]),
        pltpu.make_async_copy(ow_ref, ow.at[ctx], ls.at[2]),
        pltpu.make_async_copy(dn_ref, dn.at[ctx], ls.at[3]),
    ]
    for copy in local:
        copy.start()
    dbuf[ctx] = jnp.broadcast_to(doc_ref[...], (8, TOK))
    for j in range(1, 2 * NY):

        @pl.when(j > ctx)
        def _():
            kbuf[j] = jnp.zeros_like(kbuf[j])
            vbuf[j] = jnp.zeros_like(vbuf[j])
            dbuf[j] = jnp.zeros_like(dbuf[j])

    pl.semaphore_wait(barrier, len(partners))

    kv_ids = {}
    for k in (1, 3, 2):
        ok = y + k < NY
        kv_ids[k] = [
            send(dbuf.at[ctx], dbuf.at[ctx], "y", k, ok),
            send(k_ref.at[0], kbuf.at[ctx], "y", k, ok),
            send(v_ref.at[0], vbuf.at[ctx], "y", k, ok),
        ]
    first = core == 0
    kv_own = [
        send(dbuf.at[ctx], dbuf.at[ctx], "core", 1, first),
        send(k_ref.at[0], kbuf.at[ctx], "core", 1, first),
        send(v_ref.at[0], vbuf.at[ctx], "core", 1, first),
    ]

    def w_start(src, buf):
        half = buf.shape[1] // 2

        def part(h):
            return src.at[pl.ds(h * half, half)]

        def slot(h):
            return buf.at[ctx, pl.ds(h * half, half)]

        got = {}
        got["up", 0] = send(part(0), slot(0), "y", 1)
        got["dn", 1] = send(part(1), slot(1), "y", -1)
        got["up", 1] = send(part(1), slot(1), "y", 1)
        got["dn", 0] = send(part(0), slot(0), "y", -1)
        got["own"] = send(src, buf.at[ctx], "core", 1)
        return got

    def w_piece(buf, k, h, c):
        half = buf.shape[1] // 2
        return buf.at[wrap(y + k, NY) * 2 + c, pl.ds(h * half, half)]

    def w_turn(buf, got):
        for name, h, k in (("up", 0, -1), ("dn", 1, 1)):
            ref = w_piece(buf, k, h, core)
            recv(ref, got[name, h])
            got["far", h] = send(ref, ref, "y", -k)
            got["core", k, h] = send(ref, ref, "core", 1)

    def w_share(buf, got):
        for name, h, k in (("up", 1, -1), ("dn", 0, 1)):
            ref = w_piece(buf, k, h, core)
            recv(ref, got[name, h])
            got["core", k, h] = send(ref, ref, "core", 1)
        for h in (0, 1):
            ref = w_piece(buf, 2, h, core)
            recv(ref, got["far", h])
            got["core", 2, h] = send(ref, ref, "core", 1)

    def w_done(buf, got):
        recv(buf.at[other], got["own"])
        for k in (-1, 1, 2):
            for h in (0, 1):
                recv(w_piece(buf, k, h, 1 - core), got["core", k, h])

    ow_got = w_start(ow_ref, ow)
    gu[ctx, :, :FFL] = gate_ref[...]
    gu[ctx, :, FFL:] = up_ref[...]
    gu_got = w_start(gu.at[ctx], gu)
    dn_got = w_start(dn_ref, dn)

    row_of = lax.broadcasted_iota(jnp.int32, (LAB, TOK), 0)
    lane_of = lax.broadcasted_iota(jnp.int32, (LAB, TOK), 1)
    lab_col = jnp.zeros((LAB, TOK), jnp.int32)
    for r in range(LAB):
        lab_col = jnp.where(row_of == r, lab_ref[0, r], lab_col)
    chosen = (lane_of == lab_col).astype(F32)
    pick = chosen.astype(BF16)

    base = jnp.dot(pick, res_ref[0], preferred_element_type=F32)
    for col in range(NX * NZ):
        bx_, bz_ = block_of(col)
        bsrc[bz_, bx_] = base[:, col * HD : (col + 1) * HD]
    bz[z] = bsrc[z]
    bz_ids = {k: send(bsrc.at[wrap(z + k, NZ)], bz.at[z], "z", k) for k in range(1, NZ)}

    q_lab = jnp.dot(pick, q_ref[0], preferred_element_type=F32).astype(BF16)
    for k in range(KVH):
        qlab[k] = jnp.concatenate(
            [q_lab[:, (4 * k + g) * HD : (4 * k + g + 1) * HD] for g in range(4)], axis=0
        )

    for k in range(1, NZ):
        recv(bz.at[wrap(z - k, NZ)], bz_ids[k])
    bx[x] = bz[:, x]
    bx_ids = {k: send(bz.at[:, wrap(x + k, NX)], bx.at[x], "x", k) for k in range(1, NX)}

    for copy in local:
        copy.wait()

    bufs = (dbuf, kbuf, vbuf)
    kv_core = {}
    for k in (1, 3, 2):
        ok = y - k >= 0
        src = wrap(y - k, NY) * 2 + core

        @pl.when(ok)
        def _(k=k, src=src):
            for buf, i in zip(bufs, kv_ids[k]):
                recv(buf.at[src], i)

        kv_core[k] = [send(buf.at[src], buf.at[src], "core", 1, ok) for buf in bufs]
    for k in (1, 3, 2):
        src = wrap(y - k, NY) * 2 + 1 - core

        @pl.when(y - k >= 0)
        def _(k=k, src=src):
            for buf, i in zip(bufs, kv_core[k]):
                recv(buf.at[src], i)

    @pl.when(core == 1)
    def _():
        for buf, i in zip(bufs, kv_own):
            recv(buf.at[other], i)

    key_doc = jnp.concatenate([dbuf[j][0:1] for j in range(2 * NY)], axis=1).astype(F32)
    key_pos = lax.broadcasted_iota(jnp.int32, (1, 2 * NY * TOK), 1)
    my_doc = doc_ref[...].astype(F32)

    lab_doc = jnp.sum(chosen * my_doc, axis=1, keepdims=True)
    lab_pos = lab_col[:, 0:1] + ctx * TOK
    keep = (key_pos <= lab_pos) & (key_doc == lab_doc)
    lab_bias = jnp.where(keep, 0.0, -1e30)
    lab_bias = jnp.concatenate([lab_bias] * 4, axis=0)

    def attend(q, k, add):
        lanes = pl.ds(pl.multiple_of(k * HD, HD), HD)
        keys = kbuf[:, :, lanes].reshape(2 * NY * TOK, HD)
        values = vbuf[:, :, lanes].reshape(2 * NY * TOK, HD)
        score = nt(q, keys) * SCALE2 + add
        weight = jnp.exp2(score - jnp.max(score, axis=1, keepdims=True))
        total = jnp.sum(weight, axis=1, keepdims=True)
        return jnp.dot(weight.astype(BF16), values, preferred_element_type=F32) / total

    def lab_head(k, carry):
        plab[k] = attend(qlab[k], k, lab_bias)
        return carry

    lax.fori_loop(0, KVH, lab_head, 0)
    halves = []
    for h in range(2):
        rows = []
        for sub in range(2):
            pieces = []
            for k in (4 * h + 2 * sub, 4 * h + 2 * sub + 1):
                pieces += [plab[k, g * LAB : (g + 1) * LAB] for g in range(4)]
            rows.append(jnp.concatenate(pieces, axis=1))
        halves.append(jnp.concatenate(rows, axis=0).astype(BF16))
    a0[x, z] = halves[0]
    a1[z, x] = halves[1]

    def gather_start(b0, b1):
        return (
            {k: send(b1.at[z, x], b1.at[z, x], "x", k) for k in range(1, NX)},
            {k: send(b0.at[x, z], b0.at[x, z], "z", k) for k in range(1, NZ)},
        )

    def gather_rest(b0, b1, started, between):
        x_ids, z_ids = started
        for k in range(1, NX):
            recv(b1.at[z, wrap(x - k, NX)], x_ids[k])
        up = send(b1.at[z], b1.at[z], "z", 1)
        down = send(b1.at[z], b1.at[z], "z", -1)
        for k in range(1, NZ):
            recv(b0.at[x, wrap(z - k, NZ)], z_ids[k])
        far = {k: send(b0.at[x], b0.at[x], "x", k) for k in (1, 3, 2)}
        lo, hi = pl.ds(0, NX // 2), pl.ds(NX // 2, NX // 2)
        for step in range(1, 4):
            between(step)
            from_low, from_high = wrap(z - step, NZ), wrap(z + step, NZ)
            recv(b1.at[from_low], up)
            part = b1.at[from_low] if step < 3 else b1.at[from_low, lo]
            up = send(part, part, "z", 1)
            recv(b1.at[from_high], down)
            part = b1.at[from_high] if step < 3 else b1.at[from_high, hi]
            down = send(part, part, "z", -1)
        between(4)
        recv(b1.at[wrap(z + 4, NZ), lo], up)
        recv(b1.at[wrap(z + 4, NZ), hi], down)
        for k in (1, 3, 2):
            recv(b0.at[wrap(x - k, NX)], far[k])

    def make_bias():
        doc_col = jnp.transpose(jnp.broadcast_to(my_doc, (TOK, TOK)))[:, 0:1]
        my_pos = lax.broadcasted_iota(jnp.int32, (TOK, 1), 0) + ctx * TOK
        full = (key_pos <= my_pos) & (key_doc == doc_col)
        bias[...] = jnp.where(full, 0.0, -1e30)

    def att_heads(start, stop):
        def one(h, carry):
            lanes = pl.ds(pl.multiple_of(h * HD, HD), HD)
            out = attend(q_ref[0, :, lanes], h // 4, bias[...])
            att_ref[0, :, lanes] = out.astype(BF16)
            return carry

        lax.fori_loop(start, stop, one, 0)

    started = gather_start(a0, a1)
    make_bias()
    w_turn(ow, ow_got)
    w_share(ow, ow_got)
    for k in range(1, NX):
        recv(bx.at[wrap(x - k, NX)], bx_ids[k])

    def between_first(step):
        att_heads(4 * step - 4, 4 * step)

    gather_rest(a0, a1, started, between_first)
    w_done(ow, ow_got)

    whole = ow[...].reshape(D, HD)
    quarter = D // 4
    flat = {0: a0[...].reshape(-1, quarter), 1: a1[...].reshape(-1, quarter)}
    proj = []
    for h in range(2):
        wide = jnp.concatenate(
            [whole[(2 * h + s) * quarter : (2 * h + s + 1) * quarter] for s in range(2)], axis=1
        )
        proj.append(jnp.dot(flat[h], wide, preferred_element_type=F32))
    for col in range(NX * NZ):
        bx_, bz_ = block_of(col)
        r0, r1 = (bx_ * NZ + bz_) * 16, (bz_ * NX + bx_) * 16
        state[col * LAB : (col + 1) * LAB] = (
            bx[bx_, bz_]
            + (proj[0][r0 : r0 + 8, :HD] + proj[0][r0 + 8 : r0 + 16, HD:])
            + (proj[1][r1 : r1 + 8, :HD] + proj[1][r1 + 8 : r1 + 16, HD:])
        )

    gain = gain_ref[...].astype(F32)
    sixteen = lax.broadcasted_iota(jnp.int32, (16, HD), 0)
    for h, put in ((0, s0.at[x, z]), (1, s1.at[z, x])):
        part = state[h * 128 : (h + 1) * 128]
        put[0:128] = (part * gain).astype(BF16)
        square = jnp.sum(jnp.transpose(part * part), axis=0, keepdims=True)
        top = square.astype(BF16).astype(F32)
        mid = (square - top).astype(BF16).astype(F32)
        low = square - top - mid
        put[128:144] = jnp.where(
            sixteen == 0,
            top,
            jnp.where(sixteen == 1, mid, jnp.where(sixteen == 2, low, 0.0)),
        ).astype(BF16)

    started = gather_start(s0, s1)
    w_turn(gu, gu_got)
    w_turn(dn, dn_got)

    def between_second(step):
        att_heads(12 + 4 * step, 16 + 4 * step)

    gather_rest(s0, s1, started, between_second)
    w_share(gu, gu_got)
    w_done(gu, gu_got)

    def inv_rms(buf):
        total = jnp.zeros((16, HD), F32)
        for i in range(buf.shape[0]):
            for j in range(buf.shape[1]):
                total = total + buf[i, j, 128:144].astype(F32)
        line = jnp.sum(total, axis=0, keepdims=True)
        col = jnp.transpose(jnp.broadcast_to(line, (128, 128)))
        return lax.rsqrt(col / D + 1e-5)

    scale = jnp.concatenate([inv_rms(s0), inv_rms(s1)], axis=0)
    acc[...] = jnp.zeros_like(acc)
    for c in range(2 * NY):
        pieces = []
        for col in range(4 * c, 4 * c + 4):
            bx_, bz_ = block_of(col)
            pieces.append(jnp.concatenate([s0[bx_, bz_, 0:128], s1[bz_, bx_, 0:128]], axis=0))
        acc[...] += jnp.dot(jnp.concatenate(pieces, axis=1), gu[c], preferred_element_type=F32)
    scale = jnp.concatenate([scale] * 4, axis=1)[:, :FFL]
    gate = acc[:, :FFL] * scale
    up = acc[:, FFL:] * scale
    hidden = (gate / (1.0 + jnp.exp(-gate)) * up).astype(BF16)

    w_share(dn, dn_got)
    w_done(dn, dn_got)
    for c in range(2 * NY):
        terms = jnp.dot(hidden, dn[c], preferred_element_type=F32)
        for i in range(4):
            bx_, bz_ = block_of(4 * c + i)
            cols = terms[:, i * HD : (i + 1) * HD]
            tb0[bx_, bz_] = cols[:128].astype(BF16)
            tb1[bz_, bx_] = cols[128:].astype(BF16)

    x_ids = {k: send(tb0.at[wrap(x + k, NX)], rx0.at[x], "x", k) for k in (1, 3, 2)}
    p_id = send(tb1.at[wrap(z + 4, NZ)], rp.at[0], "z", 1)
    m_id = send(tb1.at[wrap(z - 3, NZ)], rm.at[0], "z", -1)
    for step in range(3):
        recv(rp.at[step], p_id)
        sp[step] = (rp[step].astype(F32) + tb1[wrap(z + 3 - step, NZ)].astype(F32)).astype(BF16)
        p_id = send(sp.at[step], rp.at[step + 1], "z", 1)
        if step < 2:
            recv(rm.at[step], m_id)
            sm[step] = (rm[step].astype(F32) + tb1[wrap(z - 2 + step, NZ)].astype(F32)).astype(BF16)
            m_id = send(sm.at[step], rm.at[step + 1], "z", -1)
    for k in (1, 3, 2):
        recv(rx0.at[wrap(x - k, NX)], x_ids[k])

    def add_x(i):
        total = tb0[x, i].astype(F32)
        for k in (1, 2, 3):
            total = total + rx0[wrap(x - k, NX), i].astype(F32)
        return total

    def put_x(i, carry):
        sb0[i] = add_x(i).astype(BF16)
        return carry

    lax.fori_loop(0, NZ, put_x, 0)
    z_ids = {k: send(sb0.at[wrap(z + k, NZ)], rz0.at[z], "z", k) for k in range(1, NZ)}
    recv(rm.at[2], m_id)
    recv(rp.at[3], p_id)
    sb1[...] = (tb1[z].astype(F32) + rp[3].astype(F32) + rm[2].astype(F32)).astype(BF16)
    x_ids = {k: send(sb1.at[wrap(x + k, NX)], rx1.at[x], "x", k) for k in range(1, NX)}
    branch1 = sb1[x].astype(F32)
    for k in range(1, NX):
        src = wrap(x - k, NX)
        recv(rx1.at[src], x_ids[k])
        branch1 = branch1 + rx1[src].astype(F32)
    branch0 = sb0[z].astype(F32)
    for k in range(1, NZ):
        src = wrap(z - k, NZ)
        recv(rz0.at[src], z_ids[k])
        branch0 = branch0 + rz0[src].astype(F32)
    labeled = (state[...] + jnp.concatenate([branch0, branch1], axis=0)).astype(BF16)
    labeled_ref[...] = labeled

    prx[x] = nt(jnp.broadcast_to(rw_ref[...], (16, HD)), labeled)[0:8]
    x_ids = {k: send(prx.at[x], prx.at[x], "x", k) for k in range(1, NX)}
    for k in range(1, NX):
        recv(prx.at[wrap(x - k, NX)], x_ids[k])
    prz[z] = (prx[0] + prx[1]) + (prx[2] + prx[3])
    z_ids = {k: send(prz.at[z], prz.at[z], "z", k) for k in range(1, NZ)}
    for k in range(1, NZ):
        recv(prz.at[wrap(z - k, NZ)], z_ids[k])
    total = prz[0]
    for i in range(1, NZ):
        total = total + prz[i]
    reward_ref[...] = total[0:1]

    for copy, cond in sent:
        if cond is None:
            copy.wait_send()
        else:
            pl.when(cond)(copy.wait_send)


def per_device(
    queries,
    keys,
    values,
    documents,
    residual,
    labels,
    out_weight,
    norm_gain,
    gate_weight,
    up_weight,
    down_weight,
    reward_weight,
):
    vmem = pl.BlockSpec(memory_space=pltpu.VMEM)
    hbm = pl.BlockSpec(memory_space=pl.ANY)
    smem = pl.BlockSpec(memory_space=pltpu.SMEM)
    attended, labeled, reward = pl.pallas_call(
        body,
        out_shape=(
            jax.ShapeDtypeStruct((1, TOK, D), BF16),
            jax.ShapeDtypeStruct((ROWS, HD), BF16),
            jax.ShapeDtypeStruct((1, ROWS), F32),
        ),
        in_specs=[vmem, hbm, hbm, vmem, vmem, smem, hbm, vmem, vmem, vmem, hbm, vmem],
        out_specs=(vmem, vmem, vmem),
        scratch_shapes=[
            pltpu.VMEM((8, TOK, KVH * HD), BF16),
            pltpu.VMEM((8, TOK, KVH * HD), BF16),
            pltpu.VMEM((8, 8, TOK), jnp.int32),
            pltpu.VMEM((8, 512, HD), BF16),
            pltpu.VMEM((8, 512, 2 * FFL), BF16),
            pltpu.VMEM((8, FFL, 512), BF16),
            pltpu.VMEM((TOK, 8 * TOK), F32),
            pltpu.VMEM((KVH, 4 * LAB, HD), BF16),
            pltpu.VMEM((KVH, 4 * LAB, HD), F32),
            pltpu.VMEM((NX, NZ, 16, 1024), BF16),
            pltpu.VMEM((NZ, NX, 16, 1024), BF16),
            pltpu.VMEM((NZ, NX, LAB, HD), F32),
            pltpu.VMEM((NZ, NX, LAB, HD), F32),
            pltpu.VMEM((NX, NZ, LAB, HD), F32),
            pltpu.VMEM((ROWS, HD), F32),
            pltpu.VMEM((NX, NZ, 144, HD), BF16),
            pltpu.VMEM((NZ, NX, 144, HD), BF16),
            pltpu.VMEM((ROWS, 2 * FFL), F32),
            pltpu.VMEM((NX, NZ, 128, HD), BF16),
            pltpu.VMEM((NX, NZ, 128, HD), BF16),
            pltpu.VMEM((NZ, 128, HD), BF16),
            pltpu.VMEM((NZ, 128, HD), BF16),
            pltpu.VMEM((NZ, NX, 128, HD), BF16),
            pltpu.VMEM((4, NX, 128, HD), BF16),
            pltpu.VMEM((3, NX, 128, HD), BF16),
            pltpu.VMEM((3, NX, 128, HD), BF16),
            pltpu.VMEM((2, NX, 128, HD), BF16),
            pltpu.VMEM((NX, 128, HD), BF16),
            pltpu.VMEM((NX, 128, HD), BF16),
            pltpu.VMEM((NX, 8, ROWS), F32),
            pltpu.VMEM((NZ, 8, ROWS), F32),
            pltpu.SemaphoreType.DMA((NSEM,)),
            pltpu.SemaphoreType.DMA((NSEM,)),
            pltpu.SemaphoreType.DMA((4,)),
        ],
        compiler_params=pltpu.CompilerParams(
            collective_id=0, has_side_effects=True, vmem_limit_bytes=56 * 1024 * 1024
        ),
        name="layer",
    )(
        queries,
        keys,
        values,
        documents,
        residual,
        labels,
        out_weight,
        norm_gain.reshape(1, HD),
        gate_weight,
        up_weight,
        down_weight,
        reward_weight.reshape(1, HD),
    )
    return attended, labeled, reward.reshape(ROWS)


def solution(mesh):
    return jax.shard_map(
        per_device,
        mesh=mesh,
        in_specs=(
            P(("grp", "tp"), "ctx", None),
            P(("grp", "tp"), "ctx", None),
            P(("grp", "tp"), "ctx", None),
            P(("grp", "tp"), "ctx"),
            P(("grp", "tp"), "ctx", None),
            P(("grp", "tp"), "ctx"),
            P("ctx", ("grp", "tp")),
            P(("grp", "tp")),
            P("ctx", ("grp", "tp")),
            P("ctx", ("grp", "tp")),
            P(("grp", "tp"), "ctx"),
            P(("grp", "tp")),
        ),
        out_specs=(P(("grp", "tp"), "ctx", None), P("ctx", ("grp", "tp")), P("ctx")),
        check_vma=False,
    )
```

```python
import functools
import math

import jax
import jax.numpy as jnp
from jax import lax
from jax.experimental import pallas as pl
from jax.experimental.pallas import tpu as pltpu
from jax.sharding import PartitionSpec as P

MESH = pl.DeviceIdType.MESH
NX, NY, NZ = 4, 4, 8
D, H, KVH, HD, FF = 4096, 32, 8, 128, 14336
TOK, LAB = 128, 8
ROWS = 256
FFL = 448
F32, BF16 = jnp.float32, jnp.bfloat16
SCALE2 = HD**-0.5 * math.log2(math.e)
NSEM = 288
PLAN = {
    "start": (
        ("own", "out"),
        ("own", "gu"),
        ("own", "down"),
    ),
    "keys": (
        ("first", "out", "up", 0),
        ("first", "out", "dn", 1),
        ("first", "out", "up", 1),
        ("first", "out", "dn", 0),
        ("first", "gu", "up", 0),
        ("first", "gu", "dn", 1),
    ),
    "first1": (
        ("turn", "out", "up", 0),
        ("turn", "out", "dn", 1),
        ("first", "gu", "up", 1),
        ("first", "gu", "dn", 0),
    ),
    "first3": (
        ("share", "out", "up", 1),
        ("share", "out", "dn", 0),
    ),
    "first5": (
        ("turn", "gu", "up", 0),
        ("turn", "gu", "dn", 1),
        ("share", "out", "far", 0),
        ("share", "out", "far", 1),
        ("first", "down", "up", 0),
        ("first", "down", "dn", 1),
    ),
    "second4": (
        ("turn", "down", "up", 0),
        ("turn", "down", "dn", 1),
        ("first", "down", "up", 1),
        ("first", "down", "dn", 0),
    ),
    "second5": (
        ("share", "gu", "dn", 0),
        ("share", "gu", "up", 1),
        ("share", "gu", "far", 1),
        ("share", "gu", "far", 0),
    ),
    "down": (
        ("share", "down", "up", 1),
        ("share", "down", "dn", 0),
        ("share", "down", "far", 1),
        ("share", "down", "far", 0),
    ),
}
A1 = {0: (0,), 5: (1, 2)}
A2 = {0: (3,), 5: (4, 5)}
A3 = {"start": (6,), "end": (7,)}

def block_of(col):
    grp, tp = col // 2, col % 2
    return (grp // NZ) * 2 + tp, grp % NZ


def nt(a, b):
    return lax.dot_general(a, b, (((1,), (1,)), ((), ())), preferred_element_type=F32)


def body(
    q_ref,
    k_ref,
    v_ref,
    doc_ref,
    res_ref,
    lab_ref,
    ow_ref,
    gain_ref,
    gate_ref,
    up_ref,
    dn_ref,
    rw_ref,
    att_ref,
    labeled_ref,
    reward_ref,
    kbuf,
    vbuf,
    dbuf,
    ow,
    gu,
    dn,
    bias,
    qlab,
    plab,
    a0,
    a1,
    bsrc,
    bz,
    bx,
    state,
    s0,
    s1,
    acc,
    tb0,
    rx0,
    sb0,
    rz0,
    tb1,
    rp,
    rm,
    sp,
    sm,
    sb1,
    rx1,
    prx,
    prz,
    ss,
    rs,
    ls,
):
    ctx, grp, tp = lax.axis_index("ctx"), lax.axis_index("grp"), lax.axis_index("tp")
    y, core = ctx // 2, ctx % 2
    x, z = (grp // NZ) * 2 + tp, grp % NZ
    other = y * 2 + 1 - core

    def wrap(v, n):
        return lax.rem(v + n, n)

    def dev(axis, k):
        if axis == "y":
            return {"ctx": wrap(y + k, NY) * 2 + core}
        if axis == "core":
            return {"ctx": other}
        if axis == "ctx":
            return {"ctx": wrap(ctx + k, 2 * NY)}
        if axis == "z":
            return {"grp": (x // 2) * NZ + wrap(z + k, NZ)}
        there = wrap(x + k, NX)
        return {"grp": (there // 2) * NZ + z, "tp": there % 2}

    ids = iter(range(NSEM))
    sent = []

    def send(src, dst, axis, k, cond=None, when=None):
        i = next(ids)
        copy = pltpu.make_async_remote_copy(
            src_ref=src,
            dst_ref=dst,
            send_sem=ss.at[i],
            recv_sem=rs.at[i],
            device_id=dev(axis, k),
            device_id_type=MESH,
        )
        if cond is None:
            copy.start()
        else:
            pl.when(cond)(copy.start)
        sent.append((copy, cond))
        return i

    def recv(dst, i):
        pltpu.make_async_remote_copy(
            src_ref=dst,
            dst_ref=dst,
            send_sem=ss.at[i],
            recv_sem=rs.at[i],
            device_id={"ctx": other},
            device_id_type=MESH,
        ).wait_recv()

    barrier = pltpu.get_barrier_semaphore()
    partners = [("core", 1)] + [("y", k) for k in range(1, NY)]
    partners += [("x", k) for k in range(1, NX)]
    partners += [("z", k) for k in range(1, NZ)]
    for axis, k in partners:
        pl.semaphore_signal(barrier, inc=1, device_id=dev(axis, k), device_id_type=MESH)

    local = [
        pltpu.make_async_copy(k_ref.at[0], kbuf.at[ctx], ls.at[0]),
        pltpu.make_async_copy(v_ref.at[0], vbuf.at[ctx], ls.at[1]),
        pltpu.make_async_copy(ow_ref, ow.at[ctx], ls.at[2]),
        pltpu.make_async_copy(dn_ref, dn.at[ctx], ls.at[3]),
        pltpu.make_async_copy(gate_ref, gu.at[ctx, pl.ds(0, FFL)], ls.at[4]),
        pltpu.make_async_copy(up_ref, gu.at[ctx, pl.ds(FFL, FFL)], ls.at[5]),
    ]
    for copy in local:
        copy.start()
    dbuf[ctx] = jnp.broadcast_to(doc_ref[...], (8, TOK))
    for j in range(1, 2 * NY):

        @pl.when(j > ctx)
        def _():
            kbuf[j] = jnp.zeros_like(kbuf[j])
            vbuf[j] = jnp.zeros_like(vbuf[j])
            dbuf[j] = jnp.zeros_like(dbuf[j])
    pl.semaphore_wait(barrier, len(partners))

    def halves_of(ref):
        half = ref.shape[0] // 2
        return ref.at[pl.ds(0, half)], ref.at[pl.ds(half, half)]

    kv_ids = {k: [] for k in (1, 3, 2)}
    kv_own = []
    for src, buf in ((dbuf.at[ctx], dbuf), (k_ref.at[0], kbuf), (v_ref.at[0], vbuf)):
        for k in (1, 3, 2):
            kv_ids[k].append(send(src, buf.at[ctx], "y", k, y + k < NY, y - k >= 0))
        kv_own.append(send(src, buf.at[ctx], "core", 1, core == 0, core == 1))

    weights = {
        "out": (halves_of(ow_ref), ow, {}),
        "gu": ((gate_ref, up_ref), gu, {}),
        "down": (halves_of(dn_ref), dn, {}),
    }

    def w_piece(buf, k, h, c):
        return halves_of(buf.at[wrap(y + k, NY) * 2 + c])[h]

    def w_act(act, which, name="", h=0):
        parts, buf, got = weights[which]
        if act == "first":
            slot = halves_of(buf.at[ctx])[h]
            got[name, h] = send(parts[h], slot, "y", 1 if name == "up" else -1)
        elif act == "own":
            for h in (0, 1):
                got["own", h] = send(parts[h], halves_of(buf.at[ctx])[h], "core", 1)
        else:
            k = {"up": -1, "dn": 1, "far": 2}[name]
            ref = w_piece(buf, k, h, core)
            recv(ref, got[name, h])
            if act == "turn":
                got["far", h] = send(ref, ref, "y", -k)
            got["core", k, h] = send(ref, ref, "core", 1)

    def w_done(which):
        _, buf, got = weights[which]
        for h in (0, 1):
            recv(halves_of(buf.at[other])[h], got["own", h])
        for k in (-1, 1, 2):
            for h in (0, 1):
                recv(w_piece(buf, k, h, 1 - core), got["core", k, h])

    def plan(point):
        for entry in PLAN.get(point, ()):
            w_act(*entry)

    plan("start")
    row_of = lax.broadcasted_iota(jnp.int32, (LAB, TOK), 0)
    lane_of = lax.broadcasted_iota(jnp.int32, (LAB, TOK), 1)
    lab_col = jnp.zeros((LAB, TOK), jnp.int32)
    for r in range(LAB):
        lab_col = jnp.where(row_of == r, lab_ref[0, r], lab_col)
    chosen = (lane_of == lab_col).astype(F32)
    pick = chosen.astype(BF16)
    my_doc = doc_ref[...].astype(F32)
    q_lab = jnp.dot(pick, q_ref[0], preferred_element_type=F32).astype(BF16)
    for k in range(KVH):
        qlab[k] = jnp.concatenate(
            [q_lab[:, (4 * k + g) * HD : (4 * k + g + 1) * HD] for g in range(4)], axis=0
        )
    base = jnp.dot(pick, res_ref[0], preferred_element_type=F32)
    reward_row = jnp.broadcast_to(rw_ref[...].astype(F32), (LAB, HD))
    for col in range(NX * NZ):
        bx_, bz_ = block_of(col)
        bsrc[bz_, bx_, 0:LAB] = base[:, col * HD : (col + 1) * HD]
        bsrc[bz_, bx_, LAB:] = reward_row
    bz[z] = bsrc[z]
    bz_ids = {k: send(bsrc.at[wrap(z + k, NZ)], bz.at[z], "z", k) for k in range(1, NZ)}
    for copy in local:
        copy.wait()

    def attend(q, keys, values, add):
        score = nt(q, keys) * SCALE2 + add
        top = jnp.max(score, axis=1, keepdims=True)
        weight = jnp.exp2(score - top)
        total = jnp.sum(weight, axis=1, keepdims=True)
        out = jnp.dot(weight.astype(BF16), values, preferred_element_type=F32) / total
        return out

    for k in range(1, NZ):
        recv(bz.at[wrap(z - k, NZ)], bz_ids[k])
    bx[x] = bz[:, x]
    bx_ids = {k: send(bz.at[:, wrap(x + k, NX)], bx.at[x], "x", k) for k in range(1, NX)}
    bufs = (dbuf, kbuf, vbuf)
    kv_core = {}

    def kv_turn():
        for b, buf in enumerate(bufs):
            for k in (1, 3, 2):
                ok = y - k >= 0
                ref = buf.at[wrap(y - k, NY) * 2 + core]
                pl.when(ok)(functools.partial(recv, ref, kv_ids[k][b]))
                kv_core[k, b] = send(ref, ref, "core", 1, ok, ok)

    def kv_done():
        for b, buf in enumerate(bufs):
            for k in (1, 3, 2):
                ref = buf.at[wrap(y - k, NY) * 2 + 1 - core]
                pl.when(y - k >= 0)(functools.partial(recv, ref, kv_core[k, b]))
            pl.when(core == 1)(functools.partial(recv, buf.at[other], kv_own[b]))

    kv_turn()
    plan("keys")
    kv_done()

    key_doc = jnp.concatenate([dbuf[j][0:1] for j in range(2 * NY)], axis=1).astype(F32)
    key_pos = lax.broadcasted_iota(jnp.int32, (1, 2 * NY * TOK), 1)
    lab_doc = jnp.sum(chosen * my_doc, axis=1, keepdims=True)
    keep = (key_pos <= lab_col[:, 0:1] + ctx * TOK) & (key_doc == lab_doc)
    lab_bias = jnp.concatenate([jnp.where(keep, 0.0, -1e30)] * 4, axis=0)

    def head(buf, k):
        return buf[:, :, pl.ds(k * HD, HD)].reshape(2 * NY * TOK, HD)

    for k in range(KVH):
        plab[k] = attend(qlab[k], head(kbuf, k), head(vbuf, k), lab_bias)
    halves = []
    for h in range(2):
        rows = []
        for sub in range(2):
            pieces = []
            for k in (4 * h + 2 * sub, 4 * h + 2 * sub + 1):
                pieces += [plab[k, g * LAB : (g + 1) * LAB] for g in range(4)]
            rows.append(jnp.concatenate(pieces, axis=1))
        halves.append(jnp.concatenate(rows, axis=0).astype(BF16))
    a0[x, z] = halves[0]
    a1[z, x] = halves[1]

    def gather(b0, b1, between):
        def block(k):
            return b0.at[x, wrap(z + k, NZ)]

        def group(k, i):
            return b1.at[wrap(z + k, NZ), pl.ds(i * (NX // 2), NX // 2)]

        def spread(k):
            return {j: send(block(k), block(k), "x", j) for j in (1, 3, 2)}

        own = b1.at[z, x]
        x_ids = {k: send(own, own, "x", k) for k in (1, 3, 2)}
        z_ids = {k: send(block(0), block(0), "z", k) for k in (1, 7, 2, 6, 3, 5, 4)}
        far = {0: spread(0)}
        between(0)
        for k in (1, 3, 2):
            recv(b1.at[z, wrap(x - k, NX)], x_ids[k])
        up = [send(group(0, i), group(0, i), "z", 1) for i in (0, 1)]
        down = [send(group(0, i), group(0, i), "z", -1) for i in (1, 0)][::-1]
        for step in range(1, 5):
            between(step)
            for k in (-step, step) if step < 4 else (4,):
                recv(block(k), z_ids[-k % NZ])
                far[k] = spread(k)
            for i in (0, 1):
                if step < 4 or i == 0:
                    recv(group(-step, i), up[i])
                    if step < 3 or (step == 3 and i == 0):
                        up[i] = send(group(-step, i), group(-step, i), "z", 1)
                j = 1 - i
                if step < 4 or j == 1:
                    recv(group(step, j), down[j])
                    if step < 3 or (step == 3 and j == 1):
                        down[j] = send(group(step, j), group(step, j), "z", -1)
        between(5)
        for k, ids_k in far.items():
            for j in (1, 3, 2):
                recv(b0.at[wrap(x - j, NX), wrap(z + k, NZ)], ids_k[j])

    def make_bias():
        doc_col = jnp.transpose(jnp.broadcast_to(my_doc, (TOK, TOK)))[:, 0:1]
        my_pos = lax.broadcasted_iota(jnp.int32, (TOK, 1), 0) + ctx * TOK
        full = (key_pos <= my_pos) & (key_doc == doc_col)
        bias[...] = jnp.where(full, 0.0, -1e30)

    def att_heads(start, stop):
        def one(k, carry):
            lanes = pl.ds(pl.multiple_of(k * HD, HD), HD)
            keys = kbuf[:, :, lanes].reshape(2 * NY * TOK, HD)
            values = vbuf[:, :, lanes].reshape(2 * NY * TOK, HD)
            for g in range(4):
                span = pl.ds(pl.multiple_of((4 * k + g) * HD, HD), HD)
                out = attend(q_ref[0, :, span], keys, values, bias[...])
                att_ref[0, :, span] = out.astype(BF16)
            return carry

        lax.fori_loop(start, stop, one, 0)

    plan("first")
    def between_first(step):
        plan("first%d" % step)
        if step == 0:
            make_bias()
            for k in range(1, NX):
                recv(bx.at[wrap(x - k, NX)], bx_ids[k])
        for k in A1.get(step, ()):
            att_heads(k, k + 1)

    gather(a0, a1, between_first)
    plan("out")
    w_done("out")

    whole = ow[...].reshape(D, HD)
    quarter = D // 4
    flat = {0: a0[...].reshape(-1, quarter), 1: a1[...].reshape(-1, quarter)}
    proj = []
    for h in range(2):
        wide = jnp.concatenate(
            [whole[(2 * h + s) * quarter : (2 * h + s + 1) * quarter] for s in range(2)], axis=1
        )
        proj.append(jnp.dot(flat[h], wide, preferred_element_type=F32))
    for col in range(NX * NZ):
        bx_, bz_ = block_of(col)
        r0, r1 = (bx_ * NZ + bz_) * 16, (bz_ * NX + bx_) * 16
        state[col * LAB : (col + 1) * LAB] = (
            bx[bx_, bz_, 0:LAB]
            + (proj[0][r0 : r0 + 8, :HD] + proj[0][r0 + 8 : r0 + 16, HD:])
            + (proj[1][r1 : r1 + 8, :HD] + proj[1][r1 + 8 : r1 + 16, HD:])
        )

    gain = gain_ref[...].astype(F32)
    sixteen = lax.broadcasted_iota(jnp.int32, (16, HD), 0)
    for h, put in ((0, s0.at[x, z]), (1, s1.at[z, x])):
        part = state[h * 128 : (h + 1) * 128]
        put[0:128] = (part * gain).astype(BF16)
        square = jnp.sum(jnp.transpose(part * part), axis=0, keepdims=True)
        top = square.astype(BF16).astype(F32)
        mid = (square - top).astype(BF16).astype(F32)
        low = square - top - mid
        put[128:144] = jnp.where(
            sixteen == 0,
            top,
            jnp.where(sixteen == 1, mid, jnp.where(sixteen == 2, low, 0.0)),
        ).astype(BF16)

    plan("second")

    def between_second(step):
        plan("second%d" % step)
        for k in A2.get(step, ()):
            att_heads(k, k + 1)

    gather(s0, s1, between_second)
    plan("gu")
    w_done("gu")

    def inv_rms(buf):
        total = jnp.zeros((16, HD), F32)
        for i in range(buf.shape[0]):
            for j in range(buf.shape[1]):
                total = total + buf[i, j, 128:144].astype(F32)
        line = jnp.sum(total, axis=0, keepdims=True)
        col = jnp.transpose(jnp.broadcast_to(line, (128, 128)))
        return lax.rsqrt(col / D + 1e-5)

    scale = jnp.concatenate([inv_rms(s0), inv_rms(s1)], axis=0)
    acc[...] = jnp.zeros_like(acc)
    for c in range(2 * NY):
        pieces = []
        for col in range(4 * c, 4 * c + 4):
            bx_, bz_ = block_of(col)
            pieces.append(jnp.concatenate([s0[bx_, bz_, 0:128], s1[bz_, bx_, 0:128]], axis=0))
        acc[...] += nt(jnp.concatenate(pieces, axis=1), gu[c])
    scale = jnp.concatenate([scale] * 4, axis=1)[:, :FFL]
    gate = acc[:, :FFL] * scale
    up = acc[:, FFL:] * scale
    hidden = (gate / (1.0 + jnp.exp(-gate)) * up).astype(BF16)

    plan("down")
    w_done("down")
    own_reward = jnp.broadcast_to(rw_ref[...], (16, HD))
    high = state[...].astype(BF16)
    part_reward = nt(own_reward, high) + nt(own_reward, (state[...] - high.astype(F32)).astype(BF16))
    for c in range(2 * NY):
        terms = jnp.dot(hidden, dn[c], preferred_element_type=F32).astype(BF16)
        line = [bx[block_of(4 * c + i) + (slice(LAB, None),)] for i in range(4)]
        line = jnp.concatenate(line, axis=1)
        part_reward = part_reward + nt(jnp.concatenate([line, line], axis=0).astype(BF16), terms)
        for i in range(4):
            bx_, bz_ = block_of(4 * c + i)
            cols = terms[:, i * HD : (i + 1) * HD]
            tb0[bx_, bz_] = cols[:128]
            tb1[bz_, bx_] = cols[128:]

    lo, hi = pl.ds(0, NX // 2), pl.ds(NX // 2, NX // 2)
    chains = {
        "up_lo": (1, lo, 4, rp, sp),
        "dn_hi": (-1, hi, 4, rm, sm),
        "up_hi": (1, hi, 3, rp, sp),
        "dn_lo": (-1, lo, 3, rm, sm),
    }
    hop = {}
    for name, (k, part, count, got, _) in chains.items():
        hop[name] = send(tb1.at[wrap(z + k * count, NZ), part], got.at[0, part], "z", k)
    x_ids = {}
    for d in (4, 3, -3, 2, -2, 1, -1, 0):
        there = wrap(z + d, NZ)
        for k in (1, 3, 2):
            x_ids[d, k] = send(tb0.at[wrap(x + k, NX), there], rx0.at[x, there], "x", k)
    prx[x] = part_reward[0:8]
    rx_ids = {k: send(prx.at[x], prx.at[x], "x", k) for k in range(1, NX)}
    for k in A3.get("start", ()):
        att_heads(k, k + 1)
    z_ids = {}

    def add_x(d):
        there = wrap(z + d, NZ)
        total = tb0[x, there].astype(F32)
        for k in (1, 3, 2):
            src = wrap(x - k, NX)
            recv(rx0.at[src, there], x_ids[d, k])
            total = total + rx0[src, there].astype(F32)
        return total

    def pass_on(d):
        there = wrap(z + d, NZ)
        sb0[there] = add_x(d).astype(BF16)
        z_ids[d % NZ] = send(sb0.at[there], rz0.at[z], "z", d)

    for step in range(3):
        for name, (k, part, count, got, out) in chains.items():
            if step + 1 < count:
                recv(got.at[step, part], hop[name])
                own = tb1[wrap(z + k * (count - 1 - step), NZ), part]
                out[step, part] = (got[step, part].astype(F32) + own.astype(F32)).astype(BF16)
                hop[name] = send(out.at[step, part], got.at[step + 1, part], "z", k)
        for d in ((4, 3), (-3, 2), (-2, 1))[step]:
            pass_on(d)
    pass_on(-1)
    for k in range(1, NX):
        recv(prx.at[wrap(x - k, NX)], rx_ids[k])
    prz[z] = (prx[0] + prx[1]) + (prx[2] + prx[3])
    rz_ids = {k: send(prz.at[z], prz.at[z], "z", k) for k in range(1, NZ)}
    for name, (k, part, count, got, _) in chains.items():
        recv(got.at[count - 1, part], hop[name])
    for part, last_up, last_down in ((lo, 3, 2), (hi, 2, 3)):
        pair = rp[last_up, part].astype(F32) + rm[last_down, part].astype(F32)
        sb1[part] = (tb1[z, part].astype(F32) + pair).astype(BF16)
    far_ids = {k: send(sb1.at[wrap(x + k, NX)], rx1.at[x], "x", k) for k in range(1, NX)}
    for k in A3.get("end", ()):
        att_heads(k, k + 1)
    branch1 = sb1[x].astype(F32)
    for k in range(1, NX):
        src = wrap(x - k, NX)
        recv(rx1.at[src], far_ids[k])
        branch1 = branch1 + rx1[src].astype(F32)
    branch0 = add_x(0)
    for k in range(1, NZ):
        src = wrap(z - k, NZ)
        recv(rz0.at[src], z_ids[k])
        branch0 = branch0 + rz0[src].astype(F32)
    labeled = (state[...] + jnp.concatenate([branch0, branch1], axis=0)).astype(BF16)
    labeled_ref[...] = labeled
    for k in range(1, NZ):
        recv(prz.at[wrap(z - k, NZ)], rz_ids[k])
    total = prz[0]
    for i in range(1, NZ):
        total = total + prz[i]
    reward_ref[...] = total[0:1]

    for copy, cond in sent:
        if cond is None:
            copy.wait_send()
        else:
            pl.when(cond)(copy.wait_send)


def per_device(
    queries,
    keys,
    values,
    documents,
    residual,
    labels,
    out_weight,
    norm_gain,
    gate_weight,
    up_weight,
    down_weight,
    reward_weight,
):
    vmem = pl.BlockSpec(memory_space=pltpu.VMEM)
    hbm = pl.BlockSpec(memory_space=pl.ANY)
    smem = pl.BlockSpec(memory_space=pltpu.SMEM)
    attended, labeled, reward = pl.pallas_call(
        body,
        out_shape=(
            jax.ShapeDtypeStruct((1, TOK, D), BF16),
            jax.ShapeDtypeStruct((ROWS, HD), BF16),
            jax.ShapeDtypeStruct((1, ROWS), F32),
        ),
        in_specs=[vmem, hbm, hbm, vmem, vmem, smem, hbm, vmem, hbm, hbm, hbm, vmem],
        out_specs=(vmem, vmem, vmem),
        scratch_shapes=[
            pltpu.VMEM((8, TOK, KVH * HD), BF16),
            pltpu.VMEM((8, TOK, KVH * HD), BF16),
            pltpu.VMEM((8, 8, TOK), jnp.int32),
            pltpu.VMEM((8, 512, HD), BF16),
            pltpu.VMEM((8, 2 * FFL, 512), BF16),
            pltpu.VMEM((8, FFL, 512), BF16),
            pltpu.VMEM((TOK, 8 * TOK), F32),
            pltpu.VMEM((KVH, 4 * LAB, HD), BF16),
            pltpu.VMEM((KVH, 4 * LAB, HD), F32),
            pltpu.VMEM((NX, NZ, 16, 1024), BF16),
            pltpu.VMEM((NZ, NX, 16, 1024), BF16),
            pltpu.VMEM((NZ, NX, 2 * LAB, HD), F32),
            pltpu.VMEM((NZ, NX, 2 * LAB, HD), F32),
            pltpu.VMEM((NX, NZ, 2 * LAB, HD), F32),
            pltpu.VMEM((ROWS, HD), F32),
            pltpu.VMEM((NX, NZ, 144, HD), BF16),
            pltpu.VMEM((NZ, NX, 144, HD), BF16),
            pltpu.VMEM((ROWS, 2 * FFL), F32),
            pltpu.VMEM((NX, NZ, 128, HD), BF16),
            pltpu.VMEM((NX, NZ, 128, HD), BF16),
            pltpu.VMEM((NZ, 128, HD), BF16),
            pltpu.VMEM((NZ, 128, HD), BF16),
            pltpu.VMEM((NZ, NX, 128, HD), BF16),
            pltpu.VMEM((4, NX, 128, HD), BF16),
            pltpu.VMEM((4, NX, 128, HD), BF16),
            pltpu.VMEM((3, NX, 128, HD), BF16),
            pltpu.VMEM((3, NX, 128, HD), BF16),
            pltpu.VMEM((NX, 128, HD), BF16),
            pltpu.VMEM((NX, 128, HD), BF16),
            pltpu.VMEM((NX, 8, ROWS), F32),
            pltpu.VMEM((NZ, 8, ROWS), F32),
            pltpu.SemaphoreType.DMA((NSEM,)),
            pltpu.SemaphoreType.DMA((NSEM,)),
            pltpu.SemaphoreType.DMA((6,)),
        ],
        compiler_params=pltpu.CompilerParams(
            collective_id=0, has_side_effects=True, vmem_limit_bytes=56 * 1024 * 1024
        ),
        name="layer",
    )(
        queries,
        keys,
        values,
        documents,
        residual,
        labels,
        out_weight,
        norm_gain.reshape(1, HD),
        gate_weight.T,
        up_weight.T,
        down_weight,
        reward_weight.reshape(1, HD),
    )
    return attended, labeled, reward.reshape(ROWS)


def solution(mesh):
    return jax.shard_map(
        per_device,
        mesh=mesh,
        in_specs=(
            P(("grp", "tp"), "ctx", None),
            P(("grp", "tp"), "ctx", None),
            P(("grp", "tp"), "ctx", None),
            P(("grp", "tp"), "ctx"),
            P(("grp", "tp"), "ctx", None),
            P(("grp", "tp"), "ctx"),
            P("ctx", ("grp", "tp")),
            P(("grp", "tp")),
            P("ctx", ("grp", "tp")),
            P("ctx", ("grp", "tp")),
            P(("grp", "tp"), "ctx"),
            P(("grp", "tp")),
        ),
        out_specs=(P(("grp", "tp"), "ctx", None), P("ctx", ("grp", "tp")), P("ctx")),
        check_vma=False,
    )
```

```python
import functools
import math

import jax
import jax.numpy as jnp
from jax import lax
from jax.experimental import pallas as pl
from jax.experimental.pallas import tpu as pltpu
from jax.sharding import PartitionSpec as P

MESH = pl.DeviceIdType.MESH
NX, NY, NZ = 4, 4, 8
D, H, KVH, HD, FF = 4096, 32, 8, 128, 14336
TOK, LAB = 128, 8
ROWS = 256
R0, R1 = 144, 112
AHEAD = 3
C0, C1 = 1280, 768
FFL = 448
F32, BF16 = jnp.float32, jnp.bfloat16
SCALE2 = HD**-0.5 * math.log2(math.e)
NSEM = 288
PLAN = {
    "start": (
        ("own", "out"),
        ("own", "gu"),
        ("own", "down"),
    ),
    "keys": (
        ("first", "out", "up", 0),
        ("first", "out", "dn", 1),
        ("first", "out", "up", 1),
        ("first", "out", "dn", 0),
        ("first", "gu", "up", 0),
        ("first", "gu", "dn", 1),
    ),
    "first1": (
        ("turn", "out", "up", 0),
        ("turn", "out", "dn", 1),
        ("first", "gu", "up", 1),
        ("first", "gu", "dn", 0),
    ),
    "first3": (
        ("share", "out", "up", 1),
        ("share", "out", "dn", 0),
    ),
    "first5": (
        ("turn", "gu", "up", 0),
        ("turn", "gu", "dn", 1),
        ("share", "out", "far", 0),
        ("share", "out", "far", 1),
        ("first", "down", "up", 0),
        ("first", "down", "dn", 1),
    ),
    "second4": (
        ("turn", "down", "up", 0),
        ("turn", "down", "dn", 1),
        ("first", "down", "up", 1),
        ("first", "down", "dn", 0),
    ),
    "second5": (
        ("share", "gu", "dn", 0),
        ("share", "gu", "up", 1),
        ("share", "gu", "far", 1),
        ("share", "gu", "far", 0),
    ),
    "down": (
        ("share", "down", "up", 1),
        ("share", "down", "dn", 0),
        ("share", "down", "far", 1),
        ("share", "down", "far", 0),
    ),
}
A1 = {0: (0,), 5: (1, 2)}
A2 = {0: (3,), 5: (4, 5)}
A3 = {"start": (6,), "end": (7,)}

def block_of(col):
    grp, tp = col // 2, col % 2
    return (grp // NZ) * 2 + tp, grp % NZ


def nt(a, b):
    return lax.dot_general(a, b, (((1,), (1,)), ((), ())), preferred_element_type=F32)


def body(
    q_hbm,
    k_ref,
    v_ref,
    doc_ref,
    res_hbm,
    lab_ref,
    ow_ref,
    gain_ref,
    gate_ref,
    up_ref,
    dn_ref,
    rw_ref,
    att_ref,
    labeled_ref,
    reward_ref,
    q_ref,
    res_ref,
    kbuf,
    vbuf,
    dbuf,
    ow,
    gu,
    dn,
    bias,
    qlab,
    plab,
    a0,
    a1,
    bsrc,
    bz,
    bx,
    state,
    s0,
    s1,
    acc,
    tb0,
    rx0,
    sb0,
    rz0,
    tb1,
    rp,
    rm,
    sp,
    sm,
    sb1,
    rx1,
    prx,
    prz,
    ss,
    rs,
    ls,
):
    ctx, grp, tp = lax.axis_index("ctx"), lax.axis_index("grp"), lax.axis_index("tp")
    y, core = ctx // 2, ctx % 2
    x, z = (grp // NZ) * 2 + tp, grp % NZ
    other = y * 2 + 1 - core

    def wrap(v, n):
        return lax.rem(v + n, n)

    def dev(axis, k):
        if axis == "y":
            return {"ctx": wrap(y + k, NY) * 2 + core}
        if axis == "core":
            return {"ctx": other}
        if axis == "ctx":
            return {"ctx": wrap(ctx + k, 2 * NY)}
        if axis == "z":
            return {"grp": (x // 2) * NZ + wrap(z + k, NZ)}
        there = wrap(x + k, NX)
        return {"grp": (there // 2) * NZ + z, "tp": there % 2}

    ids = iter(range(NSEM))
    sent = []

    def send(src, dst, axis, k, cond=None, when=None):
        i = next(ids)
        copy = pltpu.make_async_remote_copy(
            src_ref=src,
            dst_ref=dst,
            send_sem=ss.at[i],
            recv_sem=rs.at[i],
            device_id=dev(axis, k),
            device_id_type=MESH,
        )
        if cond is None:
            copy.start()
        else:
            pl.when(cond)(copy.start)
        sent.append((copy, cond))
        return i

    def recv(dst, i):
        pltpu.make_async_remote_copy(
            src_ref=dst,
            dst_ref=dst,
            send_sem=ss.at[i],
            recv_sem=rs.at[i],
            device_id={"ctx": other},
            device_id_type=MESH,
        ).wait_recv()

    barrier = pltpu.get_barrier_semaphore()
    partners = [("core", 1)] + [("y", k) for k in range(1, NY)]
    partners += [("x", k) for k in range(1, NX)]
    partners += [("z", k) for k in range(1, NZ)]
    for axis, k in partners:
        pl.semaphore_signal(barrier, inc=1, device_id=dev(axis, k), device_id_type=MESH)

    local = [
        pltpu.make_async_copy(q_hbm, q_ref, ls.at[6]),
        pltpu.make_async_copy(res_hbm, res_ref, ls.at[7]),
        pltpu.make_async_copy(k_ref.at[0], kbuf.at[ctx], ls.at[0]),
        pltpu.make_async_copy(v_ref.at[0], vbuf.at[ctx], ls.at[1]),
        pltpu.make_async_copy(ow_ref, ow.at[ctx], ls.at[2]),
        pltpu.make_async_copy(dn_ref, dn.at[ctx], ls.at[3]),
        pltpu.make_async_copy(gate_ref, gu.at[ctx, pl.ds(0, FFL)], ls.at[4]),
        pltpu.make_async_copy(up_ref, gu.at[ctx, pl.ds(FFL, FFL)], ls.at[5]),
    ]
    for copy in local:
        copy.start()
    dbuf[ctx] = jnp.broadcast_to(doc_ref[...], (8, TOK))
    pl.semaphore_wait(barrier, len(partners))

    def halves_of(ref):
        half = ref.shape[0] // 2
        return ref.at[pl.ds(0, half)], ref.at[pl.ds(half, half)]

    kv_ids = {k: [] for k in (1, 3, 2)}
    kv_own = []
    for src, buf in ((dbuf.at[ctx], dbuf), (k_ref.at[0], kbuf), (v_ref.at[0], vbuf)):
        for k in (1, 3, 2):
            kv_ids[k].append(send(src, buf.at[ctx], "y", k, y + k < NY, y - k >= 0))
        kv_own.append(send(src, buf.at[ctx], "core", 1, core == 0, core == 1))

    weights = {
        "out": (halves_of(ow_ref), ow, {}),
        "gu": ((gate_ref, up_ref), gu, {}),
        "down": (halves_of(dn_ref), dn, {}),
    }

    def w_piece(buf, k, h, c):
        return halves_of(buf.at[wrap(y + k, NY) * 2 + c])[h]

    def w_act(act, which, name="", h=0):
        parts, buf, got = weights[which]
        if act == "first":
            slot = halves_of(buf.at[ctx])[h]
            got[name, h] = send(parts[h], slot, "y", 1 if name == "up" else -1)
        elif act == "own":
            for h in (0, 1):
                got["own", h] = send(parts[h], halves_of(buf.at[ctx])[h], "core", 1)
        else:
            k = {"up": -1, "dn": 1, "far": 2}[name]
            ref = w_piece(buf, k, h, core)
            recv(ref, got[name, h])
            if act == "turn":
                got["far", h] = send(ref, ref, "y", -k)
            got["core", k, h] = send(ref, ref, "core", 1)

    def w_done(which):
        _, buf, got = weights[which]
        for h in (0, 1):
            recv(halves_of(buf.at[other])[h], got["own", h])
        for k in (-1, 1, 2):
            for h in (0, 1):
                recv(w_piece(buf, k, h, 1 - core), got["core", k, h])

    def plan(point):
        for entry in PLAN.get(point, ()):
            w_act(*entry)

    plan("start")
    for j in range(1, 2 * NY):

        @pl.when(j > ctx)
        def _():
            kbuf[j] = jnp.zeros_like(kbuf[j])
            vbuf[j] = jnp.zeros_like(vbuf[j])
            dbuf[j] = jnp.zeros_like(dbuf[j])
    row_of = lax.broadcasted_iota(jnp.int32, (LAB, TOK), 0)
    lane_of = lax.broadcasted_iota(jnp.int32, (LAB, TOK), 1)
    lab_col = jnp.zeros((LAB, TOK), jnp.int32)
    for r in range(LAB):
        lab_col = jnp.where(row_of == r, lab_ref[0, r], lab_col)
    chosen = (lane_of == lab_col).astype(F32)
    pick = chosen.astype(BF16)
    my_doc = doc_ref[...].astype(F32)
    for copy in local[:2]:
        copy.wait()
    q_lab = jnp.dot(pick, q_ref[0], preferred_element_type=F32).astype(BF16)
    for k in range(KVH):
        qlab[k] = jnp.concatenate(
            [q_lab[:, (4 * k + g) * HD : (4 * k + g + 1) * HD] for g in range(4)], axis=0
        )
    base = jnp.dot(pick, res_ref[0], preferred_element_type=F32)
    reward_row = jnp.broadcast_to(rw_ref[...].astype(F32), (LAB, HD))
    for col in range(NX * NZ):
        bx_, bz_ = block_of(col)
        bsrc[bz_, bx_, 0:LAB] = base[:, col * HD : (col + 1) * HD]
        bsrc[bz_, bx_, LAB:] = reward_row
    bz[z] = bsrc[z]
    bz_ids = {k: send(bsrc.at[wrap(z + k, NZ)], bz.at[z], "z", k) for k in range(1, NZ)}
    for copy in local[2:]:
        copy.wait()

    def attend(q, keys, values, add):
        score = nt(q, keys) * SCALE2 + add
        top = jnp.max(score, axis=1, keepdims=True)
        weight = jnp.exp2(score - top)
        total = jnp.sum(weight, axis=1, keepdims=True)
        out = jnp.dot(weight.astype(BF16), values, preferred_element_type=F32) / total
        return out

    for k in range(1, NZ):
        recv(bz.at[wrap(z - k, NZ)], bz_ids[k])
    bx[x] = bz[:, x]
    bx_ids = {k: send(bz.at[:, wrap(x + k, NX)], bx.at[x], "x", k) for k in range(1, NX)}
    bufs = (dbuf, kbuf, vbuf)
    kv_core = {}

    def kv_turn():
        for b, buf in enumerate(bufs):
            for k in (1, 3, 2):
                ok = y - k >= 0
                ref = buf.at[wrap(y - k, NY) * 2 + core]
                pl.when(ok)(functools.partial(recv, ref, kv_ids[k][b]))
                kv_core[k, b] = send(ref, ref, "core", 1, ok, ok)

    def kv_done():
        for b, buf in enumerate(bufs):
            for k in (1, 3, 2):
                ref = buf.at[wrap(y - k, NY) * 2 + 1 - core]
                pl.when(y - k >= 0)(functools.partial(recv, ref, kv_core[k, b]))
            pl.when(core == 1)(functools.partial(recv, buf.at[other], kv_own[b]))

    kv_turn()
    plan("keys")
    kv_done()

    key_doc = jnp.concatenate([dbuf[j][0:1] for j in range(2 * NY)], axis=1).astype(F32)
    key_pos = lax.broadcasted_iota(jnp.int32, (1, 2 * NY * TOK), 1)
    lab_doc = jnp.sum(chosen * my_doc, axis=1, keepdims=True)
    keep = (key_pos <= lab_col[:, 0:1] + ctx * TOK) & (key_doc == lab_doc)
    lab_bias = jnp.concatenate([jnp.where(keep, 0.0, -1e30)] * 4, axis=0)

    def head(buf, k):
        return buf[:, :, pl.ds(k * HD, HD)].reshape(2 * NY * TOK, HD)

    def lab_heads(start, stop):
        for k in range(start, stop):
            plab[k] = attend(qlab[k], head(kbuf, k), head(vbuf, k), lab_bias)

    def lab_part(first, wide):
        rows = []
        for top in (first, first + wide // 2):
            pieces = [plab[h // 4, h % 4 * LAB : h % 4 * LAB + LAB] for h in range(top, top + wide // 2)]
            rows.append(jnp.concatenate(pieces, axis=1))
        return jnp.concatenate(rows, axis=0).astype(BF16)

    split = 2 * C0 // HD
    lab_heads(split // 4, KVH)
    a1[z, x] = lab_part(split, 2 * C1 // HD)
    a1_ids = {k: send(a1.at[z, x], a1.at[z, x], "x", k) for k in (1, 3, 2)}
    lab_heads(0, split // 4)
    a0[x, z] = lab_part(0, 2 * C0 // HD)

    def gather(b0, b1, between, x_ids=None):
        def block(k):
            return b0.at[x, wrap(z + k, NZ)]

        def group(k, i):
            return b1.at[wrap(z + k, NZ), pl.ds(i * (NX // 2), NX // 2)]

        def spread(k):
            return {j: send(block(k), block(k), "x", j) for j in (1, 3, 2)}

        own = b1.at[z, x]
        if x_ids is None:
            x_ids = {k: send(own, own, "x", k) for k in (1, 3, 2)}
        z_ids = {k: send(block(0), block(0), "z", k) for k in (1, 7, 2, 6)}
        far = {0: spread(0)}
        between(0)
        for k in (1, 3, 2):
            recv(b1.at[z, wrap(x - k, NX)], x_ids[k])
        up = [send(group(0, i), group(0, i), "z", 1) for i in (0, 1)]
        down = [send(group(0, i), group(0, i), "z", -1) for i in (1, 0)][::-1]
        for step in range(1, 5):
            between(step)
            if step == 1:
                z_ids.update({k: send(block(0), block(0), "z", k) for k in (3, 5, 4)})
            for k in (-step, step) if step < 4 else (4,):
                recv(block(k), z_ids[-k % NZ])
                far[k] = spread(k)
            for i in (0, 1):
                if step < 4 or i == 0:
                    recv(group(-step, i), up[i])
                    if step < 3 or (step == 3 and i == 0):
                        up[i] = send(group(-step, i), group(-step, i), "z", 1)
                j = 1 - i
                if step < 4 or j == 1:
                    recv(group(step, j), down[j])
                    if step < 3 or (step == 3 and j == 1):
                        down[j] = send(group(step, j), group(step, j), "z", -1)
        between(5)
        for k, ids_k in far.items():
            for j in (1, 3, 2):
                recv(b0.at[wrap(x - j, NX), wrap(z + k, NZ)], ids_k[j])

    def make_bias():
        doc_col = jnp.transpose(jnp.broadcast_to(my_doc, (TOK, TOK)))[:, 0:1]
        my_pos = lax.broadcasted_iota(jnp.int32, (TOK, 1), 0) + ctx * TOK
        full = (key_pos <= my_pos) & (key_doc == doc_col)
        bias[...] = jnp.where(full, 0.0, -1e30)

    def att_heads(start, stop):
        def one(k, carry):
            lanes = pl.ds(pl.multiple_of(k * HD, HD), HD)
            keys = kbuf[:, :, lanes].reshape(2 * NY * TOK, HD)
            values = vbuf[:, :, lanes].reshape(2 * NY * TOK, HD)
            for g in range(4):
                span = pl.ds(pl.multiple_of((4 * k + g) * HD, HD), HD)
                out = attend(q_ref[0, :, span], keys, values, bias[...])
                att_ref[0, :, span] = out.astype(BF16)
            return carry

        lax.fori_loop(start, stop, one, 0)

    plan("first")
    def between_first(step):
        plan("first%d" % step)
        if step == 0:
            make_bias()
            for k in range(1, NX):
                recv(bx.at[wrap(x - k, NX)], bx_ids[k])
        for k in A1.get(step, ()):
            att_heads(k, k + 1)

    gather(a0, a1, between_first, a1_ids)
    plan("out")
    w_done("out")

    whole = ow[...].reshape(D, HD)
    proj = []
    for buf, first, wide in ((a0, 0, C0), (a1, 2 * C0, C1)):
        pair = [whole[first + i * wide : first + (i + 1) * wide] for i in range(2)]
        pair = jnp.concatenate(pair, axis=1)
        proj.append(jnp.dot(buf[...].reshape(-1, wide), pair, preferred_element_type=F32))
    for col in range(NX * NZ):
        bx_, bz_ = block_of(col)
        r0, r1 = (bx_ * NZ + bz_) * 16, (bz_ * NX + bx_) * 16
        state[col * LAB : (col + 1) * LAB] = (
            bx[bx_, bz_, 0:LAB]
            + (proj[0][r0 : r0 + 8, :HD] + proj[0][r0 + 8 : r0 + 16, HD:])
            + (proj[1][r1 : r1 + 8, :HD] + proj[1][r1 + 8 : r1 + 16, HD:])
        )

    gain = gain_ref[...].astype(F32)
    sixteen = lax.broadcasted_iota(jnp.int32, (16, HD), 0)
    scaled = (state[...] * gain).astype(BF16)
    s1[z, x] = scaled[R0:]
    s0[x, z, 0:R0] = scaled[:R0]
    sums = jnp.zeros((16, HD), F32)
    for h in range(2):
        part = state[h * 128 : (h + 1) * 128]
        square = jnp.sum(jnp.transpose(part * part), axis=0, keepdims=True)
        top = square.astype(BF16).astype(F32)
        mid = (square - top).astype(BF16).astype(F32)
        for i, value in enumerate((top, mid, square - top - mid)):
            sums = jnp.where(sixteen == 3 * h + i, value, sums)
    s0[x, z, R0:] = sums.astype(BF16)

    plan("second")

    def between_second(step):
        plan("second%d" % step)
        for k in A2.get(step, ()):
            att_heads(k, k + 1)

    gather(s0, s1, between_second)
    plan("gu")
    w_done("gu")

    total = jnp.zeros((16, HD), F32)
    for i in range(NX):
        for j in range(NZ):
            total = total + s0[i, j, R0:].astype(F32)
    scale = []
    for h in range(2):
        line = jnp.sum(total[3 * h : 3 * h + 3], axis=0, keepdims=True)
        scale.append(lax.rsqrt(jnp.transpose(jnp.broadcast_to(line, (128, 128))) / D + 1e-5))
    scale = jnp.concatenate(scale, axis=0)
    acc[...] = jnp.zeros_like(acc)
    for c in range(2 * NY):
        pieces = []
        for col in range(4 * c, 4 * c + 4):
            bx_, bz_ = block_of(col)
            pieces.append(jnp.concatenate([s0[bx_, bz_, 0:R0], s1[bz_, bx_]], axis=0))
        acc[...] += nt(jnp.concatenate(pieces, axis=1), gu[c])
    scale = jnp.concatenate([scale] * 4, axis=1)[:, :FFL]
    gate = acc[:, :FFL] * scale
    up = acc[:, FFL:] * scale
    hidden = (gate / (1.0 + jnp.exp(-gate)) * up).astype(BF16)

    plan("down")
    w_done("down")
    own_reward = jnp.broadcast_to(rw_ref[...], (16, HD))
    high = state[...].astype(BF16)
    part_reward = nt(own_reward, high) + nt(own_reward, (state[...] - high.astype(F32)).astype(BF16))
    for c in range(2 * NY):
        terms = jnp.dot(hidden, dn[c], preferred_element_type=F32).astype(BF16)
        line = [bx[block_of(4 * c + i) + (slice(LAB, None),)] for i in range(4)]
        line = jnp.concatenate(line, axis=1)
        part_reward = part_reward + nt(jnp.concatenate([line, line], axis=0).astype(BF16), terms)
        for i in range(4):
            bx_, bz_ = block_of(4 * c + i)
            cols = terms[:, i * HD : (i + 1) * HD]
            tb0[bx_, bz_] = cols[:R0]
            tb1[bz_, bx_] = cols[R0:]

    lo, hi = pl.ds(0, NX // 2), pl.ds(NX // 2, NX // 2)
    chains = {
        "up_lo": (1, lo, 4, rp, sp),
        "dn_hi": (-1, hi, 4, rm, sm),
        "up_hi": (1, hi, 3, rp, sp),
        "dn_lo": (-1, lo, 3, rm, sm),
    }
    hop = {}
    for name, (k, part, count, got, _) in chains.items():
        hop[name] = send(tb1.at[wrap(z + k * count, NZ), part], got.at[0, part], "z", k)
    x_ids = {}
    order = (4, 3, -3, 2, -2, 1, -1, 0)

    def send_x(d):
        there = wrap(z + d, NZ)
        for k in (1, 3, 2):
            x_ids[d, k] = send(tb0.at[wrap(x + k, NX), there], rx0.at[x, there], "x", k)

    for d in order[:AHEAD]:
        send_x(d)
    prx[x] = part_reward[0:8]
    rx_ids = {k: send(prx.at[x], prx.at[x], "x", k) for k in range(1, NX)}
    for k in A3.get("start", ()):
        att_heads(k, k + 1)
    z_ids = {}

    def add_x(d):
        there = wrap(z + d, NZ)
        total = tb0[x, there].astype(F32)
        for k in (1, 3, 2):
            src = wrap(x - k, NX)
            recv(rx0.at[src, there], x_ids[d, k])
            total = total + rx0[src, there].astype(F32)
        if d in order[:-AHEAD]:
            send_x(order[order.index(d) + AHEAD])
        return total

    def pass_on(d):
        there = wrap(z + d, NZ)
        sb0[there] = add_x(d).astype(BF16)
        z_ids[d % NZ] = send(sb0.at[there], rz0.at[z], "z", d)

    for step in range(3):
        for name, (k, part, count, got, out) in chains.items():
            if step + 1 < count:
                recv(got.at[step, part], hop[name])
                own = tb1[wrap(z + k * (count - 1 - step), NZ), part]
                out[step, part] = (got[step, part].astype(F32) + own.astype(F32)).astype(BF16)
                hop[name] = send(out.at[step, part], got.at[step + 1, part], "z", k)
        for d in ((4, 3), (-3, 2), (-2, 1))[step]:
            pass_on(d)
    pass_on(-1)
    for k in range(1, NX):
        recv(prx.at[wrap(x - k, NX)], rx_ids[k])
    prz[z] = (prx[0] + prx[1]) + (prx[2] + prx[3])
    rz_ids = {k: send(prz.at[z], prz.at[z], "z", k) for k in range(1, NZ)}
    for name, (k, part, count, got, _) in chains.items():
        recv(got.at[count - 1, part], hop[name])
    for part, last_up, last_down in ((lo, 3, 2), (hi, 2, 3)):
        pair = rp[last_up, part].astype(F32) + rm[last_down, part].astype(F32)
        sb1[part] = (tb1[z, part].astype(F32) + pair).astype(BF16)
    far_ids = {k: send(sb1.at[wrap(x + k, NX)], rx1.at[x], "x", k) for k in range(1, NX)}
    for k in A3.get("end", ()):
        att_heads(k, k + 1)
    branch1 = sb1[x].astype(F32)
    for k in range(1, NX):
        src = wrap(x - k, NX)
        recv(rx1.at[src], far_ids[k])
        branch1 = branch1 + rx1[src].astype(F32)
    branch0 = add_x(0)
    for k in range(1, NZ):
        src = wrap(z - k, NZ)
        recv(rz0.at[src], z_ids[k])
        branch0 = branch0 + rz0[src].astype(F32)
    labeled = (state[...] + jnp.concatenate([branch0, branch1], axis=0)).astype(BF16)
    labeled_ref[...] = labeled
    for k in range(1, NZ):
        recv(prz.at[wrap(z - k, NZ)], rz_ids[k])
    total = prz[0]
    for i in range(1, NZ):
        total = total + prz[i]
    reward_ref[...] = total[0:1]

    for copy, cond in sent:
        if cond is None:
            copy.wait_send()
        else:
            pl.when(cond)(copy.wait_send)


def per_device(
    queries,
    keys,
    values,
    documents,
    residual,
    labels,
    out_weight,
    norm_gain,
    gate_weight,
    up_weight,
    down_weight,
    reward_weight,
):
    vmem = pl.BlockSpec(memory_space=pltpu.VMEM)
    hbm = pl.BlockSpec(memory_space=pl.ANY)
    smem = pl.BlockSpec(memory_space=pltpu.SMEM)
    attended, labeled, reward = pl.pallas_call(
        body,
        out_shape=(
            jax.ShapeDtypeStruct((1, TOK, D), BF16),
            jax.ShapeDtypeStruct((ROWS, HD), BF16),
            jax.ShapeDtypeStruct((1, ROWS), F32),
        ),
        in_specs=[hbm, hbm, hbm, vmem, hbm, smem, hbm, vmem, hbm, hbm, hbm, vmem],
        out_specs=(vmem, vmem, vmem),
        scratch_shapes=[
            pltpu.VMEM((1, TOK, D), BF16),
            pltpu.VMEM((1, TOK, D), BF16),
            pltpu.VMEM((8, TOK, KVH * HD), BF16),
            pltpu.VMEM((8, TOK, KVH * HD), BF16),
            pltpu.VMEM((8, 8, TOK), jnp.int32),
            pltpu.VMEM((8, 512, HD), BF16),
            pltpu.VMEM((8, 2 * FFL, 512), BF16),
            pltpu.VMEM((8, FFL, 512), BF16),
            pltpu.VMEM((TOK, 8 * TOK), F32),
            pltpu.VMEM((KVH, 4 * LAB, HD), BF16),
            pltpu.VMEM((KVH, 4 * LAB, HD), F32),
            pltpu.VMEM((NX, NZ, 16, C0), BF16),
            pltpu.VMEM((NZ, NX, 16, C1), BF16),
            pltpu.VMEM((NZ, NX, 2 * LAB, HD), F32),
            pltpu.VMEM((NZ, NX, 2 * LAB, HD), F32),
            pltpu.VMEM((NX, NZ, 2 * LAB, HD), F32),
            pltpu.VMEM((ROWS, HD), F32),
            pltpu.VMEM((NX, NZ, R0 + 16, HD), BF16),
            pltpu.VMEM((NZ, NX, R1, HD), BF16),
            pltpu.VMEM((ROWS, 2 * FFL), F32),
            pltpu.VMEM((NX, NZ, R0, HD), BF16),
            pltpu.VMEM((NX, NZ, R0, HD), BF16),
            pltpu.VMEM((NZ, R0, HD), BF16),
            pltpu.VMEM((NZ, R0, HD), BF16),
            pltpu.VMEM((NZ, NX, R1, HD), BF16),
            pltpu.VMEM((4, NX, R1, HD), BF16),
            pltpu.VMEM((4, NX, R1, HD), BF16),
            pltpu.VMEM((3, NX, R1, HD), BF16),
            pltpu.VMEM((3, NX, R1, HD), BF16),
            pltpu.VMEM((NX, R1, HD), BF16),
            pltpu.VMEM((NX, R1, HD), BF16),
            pltpu.VMEM((NX, 8, ROWS), F32),
            pltpu.VMEM((NZ, 8, ROWS), F32),
            pltpu.SemaphoreType.DMA((NSEM,)),
            pltpu.SemaphoreType.DMA((NSEM,)),
            pltpu.SemaphoreType.DMA((8,)),
        ],
        compiler_params=pltpu.CompilerParams(
            collective_id=0, has_side_effects=True, vmem_limit_bytes=56 * 1024 * 1024
        ),
        name="layer",
    )(
        queries,
        keys,
        values,
        documents,
        residual,
        labels,
        out_weight,
        norm_gain.reshape(1, HD),
        gate_weight.T,
        up_weight.T,
        down_weight,
        reward_weight.reshape(1, HD),
    )
    return attended, labeled, reward.reshape(ROWS)


def solution(mesh):
    return jax.shard_map(
        per_device,
        mesh=mesh,
        in_specs=(
            P(("grp", "tp"), "ctx", None),
            P(("grp", "tp"), "ctx", None),
            P(("grp", "tp"), "ctx", None),
            P(("grp", "tp"), "ctx"),
            P(("grp", "tp"), "ctx", None),
            P(("grp", "tp"), "ctx"),
            P("ctx", ("grp", "tp")),
            P(("grp", "tp")),
            P("ctx", ("grp", "tp")),
            P("ctx", ("grp", "tp")),
            P(("grp", "tp"), "ctx"),
            P(("grp", "tp")),
        ),
        out_specs=(P(("grp", "tp"), "ctx", None), P("ctx", ("grp", "tp")), P("ctx")),
        check_vma=False,
    )
```

```python
import functools
import math

import jax
import jax.numpy as jnp
from jax import lax
from jax.experimental import pallas as pl
from jax.experimental.pallas import tpu as pltpu
from jax.sharding import PartitionSpec as P

MESH = pl.DeviceIdType.MESH
NX, NY, NZ = 4, 4, 8
D, H, KVH, HD, FF = 4096, 32, 8, 128, 14336
TOK, LAB = 128, 8
ROWS = 256
R0, R1 = 160, 96
AHEAD = 3
C0, C1 = 1280, 768
FFL = 448
F32, BF16 = jnp.float32, jnp.bfloat16
SCALE2 = HD**-0.5 * math.log2(math.e)
NSEM = 288
PLAN = {
    "start": (
        ("own", "out"),
        ("own", "gu"),
        ("own", "down"),
    ),
    "keys": (
        ("first", "out", "up", 0),
        ("first", "out", "dn", 1),
        ("first", "out", "up", 1),
        ("first", "out", "dn", 0),
        ("first", "gu", "up", 0),
        ("first", "gu", "dn", 1),
    ),
    "first1": (
        ("turn", "out", "up", 0),
        ("turn", "out", "dn", 1),
        ("first", "gu", "up", 1),
        ("first", "gu", "dn", 0),
    ),
    "first3": (
        ("share", "out", "up", 1),
        ("share", "out", "dn", 0),
    ),
    "first5": (
        ("turn", "gu", "up", 0),
        ("turn", "gu", "dn", 1),
        ("share", "out", "far", 0),
        ("share", "out", "far", 1),
        ("first", "down", "up", 0),
        ("first", "down", "dn", 1),
        ("first", "down", "up", 1),
        ("first", "down", "dn", 0),
    ),
    "second4": (
        ("turn", "down", "up", 0),
        ("turn", "down", "dn", 1),
    ),
    "second5": (
        ("share", "gu", "dn", 0),
        ("share", "gu", "up", 1),
        ("share", "gu", "far", 1),
        ("share", "gu", "far", 0),
    ),
    "down": (
        ("share", "down", "up", 1),
        ("share", "down", "dn", 0),
        ("share", "down", "far", 1),
        ("share", "down", "far", 0),
    ),
}
A1 = {0: (0,), 5: (1, 2)}
A2 = {0: (3,), 5: (4, 5)}
A3 = {"start": (6,), "end": (7,)}

def block_of(col):
    grp, tp = col // 2, col % 2
    return (grp // NZ) * 2 + tp, grp % NZ


def nt(a, b):
    return lax.dot_general(a, b, (((1,), (1,)), ((), ())), preferred_element_type=F32)


def body(
    q_hbm,
    k_ref,
    v_ref,
    doc_ref,
    res_hbm,
    lab_ref,
    ow_ref,
    gain_ref,
    gate_ref,
    up_ref,
    dn_ref,
    rw_ref,
    att_ref,
    labeled_ref,
    reward_ref,
    q_ref,
    res_ref,
    kbuf,
    vbuf,
    dbuf,
    ow,
    gu,
    dn,
    bias,
    qlab,
    plab,
    a0,
    a1,
    bsrc,
    bz,
    bx,
    state,
    s0,
    s1,
    acc,
    tb0,
    rx0,
    sb0,
    rz0,
    tb1,
    rp,
    rm,
    sp,
    sm,
    sb1,
    rx1,
    prx,
    prz,
    ss,
    rs,
    ls,
):
    ctx, grp, tp = lax.axis_index("ctx"), lax.axis_index("grp"), lax.axis_index("tp")
    y, core = ctx // 2, ctx % 2
    x, z = (grp // NZ) * 2 + tp, grp % NZ
    other = y * 2 + 1 - core

    def wrap(v, n):
        return lax.rem(v + n, n)

    def dev(axis, k):
        if axis == "y":
            return {"ctx": wrap(y + k, NY) * 2 + core}
        if axis == "core":
            return {"ctx": other}
        if axis == "ctx":
            return {"ctx": wrap(ctx + k, 2 * NY)}
        if axis == "z":
            return {"grp": (x // 2) * NZ + wrap(z + k, NZ)}
        there = wrap(x + k, NX)
        return {"grp": (there // 2) * NZ + z, "tp": there % 2}

    ids = iter(range(NSEM))
    sent = []

    def send(src, dst, axis, k, cond=None, when=None):
        i = next(ids)
        copy = pltpu.make_async_remote_copy(
            src_ref=src,
            dst_ref=dst,
            send_sem=ss.at[i],
            recv_sem=rs.at[i],
            device_id=dev(axis, k),
            device_id_type=MESH,
        )
        if cond is None:
            copy.start()
        else:
            pl.when(cond)(copy.start)
        sent.append((copy, cond))
        return i

    def recv(dst, i):
        pltpu.make_async_remote_copy(
            src_ref=dst,
            dst_ref=dst,
            send_sem=ss.at[i],
            recv_sem=rs.at[i],
            device_id={"ctx": other},
            device_id_type=MESH,
        ).wait_recv()

    barrier = pltpu.get_barrier_semaphore()
    partners = [("core", 1)] + [("y", k) for k in range(1, NY)]
    partners += [("x", k) for k in range(1, NX)]
    partners += [("z", k) for k in range(1, NZ)]
    for axis, k in partners:
        pl.semaphore_signal(barrier, inc=1, device_id=dev(axis, k), device_id_type=MESH)

    local = [
        pltpu.make_async_copy(q_hbm, q_ref, ls.at[6]),
        pltpu.make_async_copy(res_hbm, res_ref, ls.at[7]),
        pltpu.make_async_copy(k_ref.at[0], kbuf.at[ctx], ls.at[0]),
        pltpu.make_async_copy(v_ref.at[0], vbuf.at[ctx], ls.at[1]),
        pltpu.make_async_copy(ow_ref, ow.at[ctx], ls.at[2]),
        pltpu.make_async_copy(dn_ref, dn.at[ctx], ls.at[3]),
        pltpu.make_async_copy(gate_ref, gu.at[ctx, pl.ds(0, FFL)], ls.at[4]),
        pltpu.make_async_copy(up_ref, gu.at[ctx, pl.ds(FFL, FFL)], ls.at[5]),
    ]
    for copy in local:
        copy.start()
    dbuf[ctx] = jnp.broadcast_to(doc_ref[...], (8, TOK))
    pl.semaphore_wait(barrier, len(partners))

    def halves_of(ref):
        half = ref.shape[0] // 2
        return ref.at[pl.ds(0, half)], ref.at[pl.ds(half, half)]

    kv_ids = {k: [] for k in (1, 3, 2)}
    kv_own = []
    for src, buf in ((dbuf.at[ctx], dbuf), (k_ref.at[0], kbuf), (v_ref.at[0], vbuf)):
        for k in (1, 3, 2):
            kv_ids[k].append(send(src, buf.at[ctx], "y", k, y + k < NY, y - k >= 0))
        kv_own.append(send(src, buf.at[ctx], "core", 1, core == 0, core == 1))

    weights = {
        "out": (halves_of(ow_ref), ow, {}),
        "gu": ((gate_ref, up_ref), gu, {}),
        "down": (halves_of(dn_ref), dn, {}),
    }

    def w_piece(buf, k, h, c):
        return halves_of(buf.at[wrap(y + k, NY) * 2 + c])[h]

    def w_act(act, which, name="", h=0):
        parts, buf, got = weights[which]
        if act == "first":
            slot = halves_of(buf.at[ctx])[h]
            got[name, h] = send(parts[h], slot, "y", 1 if name == "up" else -1)
        elif act == "own":
            for h in (0, 1):
                got["own", h] = send(parts[h], halves_of(buf.at[ctx])[h], "core", 1)
        else:
            k = {"up": -1, "dn": 1, "far": 2}[name]
            ref = w_piece(buf, k, h, core)
            recv(ref, got[name, h])
            if act == "turn":
                got["far", h] = send(ref, ref, "y", -k)
            got["core", k, h] = send(ref, ref, "core", 1)

    def w_done(which):
        _, buf, got = weights[which]
        for h in (0, 1):
            recv(halves_of(buf.at[other])[h], got["own", h])
        for k in (-1, 1, 2):
            for h in (0, 1):
                recv(w_piece(buf, k, h, 1 - core), got["core", k, h])

    def plan(point):
        for entry in PLAN.get(point, ()):
            w_act(*entry)

    plan("start")
    for j in range(1, 2 * NY):

        @pl.when(j > ctx)
        def _():
            kbuf[j] = jnp.zeros_like(kbuf[j])
            vbuf[j] = jnp.zeros_like(vbuf[j])
            dbuf[j] = jnp.zeros_like(dbuf[j])
    row_of = lax.broadcasted_iota(jnp.int32, (LAB, TOK), 0)
    lane_of = lax.broadcasted_iota(jnp.int32, (LAB, TOK), 1)
    lab_col = jnp.zeros((LAB, TOK), jnp.int32)
    for r in range(LAB):
        lab_col = jnp.where(row_of == r, lab_ref[0, r], lab_col)
    chosen = (lane_of == lab_col).astype(F32)
    pick = chosen.astype(BF16)
    my_doc = doc_ref[...].astype(F32)
    for copy in local[:2]:
        copy.wait()
    q_lab = jnp.dot(pick, q_ref[0], preferred_element_type=F32).astype(BF16)
    for k in range(KVH):
        qlab[k] = jnp.concatenate(
            [q_lab[:, (4 * k + g) * HD : (4 * k + g + 1) * HD] for g in range(4)], axis=0
        )
    base = jnp.dot(pick, res_ref[0], preferred_element_type=F32)
    reward_row = jnp.broadcast_to(rw_ref[...].astype(F32), (LAB, HD))
    for col in range(NX * NZ):
        bx_, bz_ = block_of(col)
        bsrc[bz_, bx_, 0:LAB] = base[:, col * HD : (col + 1) * HD]
        bsrc[bz_, bx_, LAB:] = reward_row
    bz[z] = bsrc[z]
    bz_ids = {k: send(bsrc.at[wrap(z + k, NZ)], bz.at[z], "z", k) for k in range(1, NZ)}
    for copy in local[2:]:
        copy.wait()

    def attend(q, keys, values, add):
        score = nt(q, keys) * SCALE2 + add
        top = jnp.max(score, axis=1, keepdims=True)
        weight = jnp.exp2(score - top)
        total = jnp.sum(weight, axis=1, keepdims=True)
        out = jnp.dot(weight.astype(BF16), values, preferred_element_type=F32) / total
        return out

    for k in range(1, NZ):
        recv(bz.at[wrap(z - k, NZ)], bz_ids[k])
    bx[x] = bz[:, x]
    bx_ids = {k: send(bz.at[:, wrap(x + k, NX)], bx.at[x], "x", k) for k in range(1, NX)}
    bufs = (dbuf, kbuf, vbuf)
    kv_core = {}

    def kv_turn():
        for b, buf in enumerate(bufs):
            for k in (1, 3, 2):
                ok = y - k >= 0
                ref = buf.at[wrap(y - k, NY) * 2 + core]
                pl.when(ok)(functools.partial(recv, ref, kv_ids[k][b]))
                kv_core[k, b] = send(ref, ref, "core", 1, ok, ok)

    def kv_done():
        for b, buf in enumerate(bufs):
            for k in (1, 3, 2):
                ref = buf.at[wrap(y - k, NY) * 2 + 1 - core]
                pl.when(y - k >= 0)(functools.partial(recv, ref, kv_core[k, b]))
            pl.when(core == 1)(functools.partial(recv, buf.at[other], kv_own[b]))

    kv_turn()
    plan("keys")
    kv_done()

    key_doc = jnp.concatenate([dbuf[j][0:1] for j in range(2 * NY)], axis=1).astype(F32)
    key_pos = lax.broadcasted_iota(jnp.int32, (1, 2 * NY * TOK), 1)
    lab_doc = jnp.sum(chosen * my_doc, axis=1, keepdims=True)
    keep = (key_pos <= lab_col[:, 0:1] + ctx * TOK) & (key_doc == lab_doc)
    lab_bias = jnp.concatenate([jnp.where(keep, 0.0, -1e30)] * 4, axis=0)

    def head(buf, k):
        return buf[:, :, pl.ds(k * HD, HD)].reshape(2 * NY * TOK, HD)

    def lab_heads(start, stop):
        for k in range(start, stop):
            plab[k] = attend(qlab[k], head(kbuf, k), head(vbuf, k), lab_bias)

    def lab_part(first, wide):
        rows = []
        for top in (first, first + wide // 2):
            pieces = [plab[h // 4, h % 4 * LAB : h % 4 * LAB + LAB] for h in range(top, top + wide // 2)]
            rows.append(jnp.concatenate(pieces, axis=1))
        return jnp.concatenate(rows, axis=0).astype(BF16)

    split = 2 * C0 // HD
    lab_heads(split // 4, KVH)
    a1[z, x] = lab_part(split, 2 * C1 // HD)
    a1_ids = {k: send(a1.at[z, x], a1.at[z, x], "x", k) for k in (1, 3, 2)}
    lab_heads(0, split // 4)
    a0[x, z] = lab_part(0, 2 * C0 // HD)

    def gather(b0, b1, between, x_ids=None):
        def block(k):
            return b0.at[x, wrap(z + k, NZ)]

        def group(k, i):
            return b1.at[wrap(z + k, NZ), pl.ds(i * (NX // 2), NX // 2)]

        def spread(k):
            return {j: send(block(k), block(k), "x", j) for j in (1, 3, 2)}

        own = b1.at[z, x]
        if x_ids is None:
            x_ids = {k: send(own, own, "x", k) for k in (1, 3, 2)}
        z_ids = {k: send(block(0), block(0), "z", k) for k in (1, 7, 2, 6)}
        far = {0: spread(0)}
        between(0)
        for k in (1, 3, 2):
            recv(b1.at[z, wrap(x - k, NX)], x_ids[k])
        up = [send(group(0, i), group(0, i), "z", 1) for i in (0, 1)]
        down = [send(group(0, i), group(0, i), "z", -1) for i in (1, 0)][::-1]
        for step in range(1, 5):
            between(step)
            if step == 1:
                z_ids.update({k: send(block(0), block(0), "z", k) for k in (3, 5, 4)})
            for k in (-step, step) if step < 4 else (4,):
                recv(block(k), z_ids[-k % NZ])
                far[k] = spread(k)
            for i in (0, 1):
                if step < 4 or i == 0:
                    recv(group(-step, i), up[i])
                    if step < 3 or (step == 3 and i == 0):
                        up[i] = send(group(-step, i), group(-step, i), "z", 1)
                j = 1 - i
                if step < 4 or j == 1:
                    recv(group(step, j), down[j])
                    if step < 3 or (step == 3 and j == 1):
                        down[j] = send(group(step, j), group(step, j), "z", -1)
        between(5)
        for k, ids_k in far.items():
            for j in (1, 3, 2):
                recv(b0.at[wrap(x - j, NX), wrap(z + k, NZ)], ids_k[j])

    def make_bias():
        doc_col = jnp.transpose(jnp.broadcast_to(my_doc, (TOK, TOK)))[:, 0:1]
        my_pos = lax.broadcasted_iota(jnp.int32, (TOK, 1), 0) + ctx * TOK
        full = (key_pos <= my_pos) & (key_doc == doc_col)
        bias[...] = jnp.where(full, 0.0, -1e30)

    def att_heads(start, stop):
        def one(k, carry):
            lanes = pl.ds(pl.multiple_of(k * HD, HD), HD)
            keys = kbuf[:, :, lanes].reshape(2 * NY * TOK, HD)
            values = vbuf[:, :, lanes].reshape(2 * NY * TOK, HD)
            for g in range(4):
                span = pl.ds(pl.multiple_of((4 * k + g) * HD, HD), HD)
                out = attend(q_ref[0, :, span], keys, values, bias[...])
                att_ref[0, :, span] = out.astype(BF16)
            return carry

        lax.fori_loop(start, stop, one, 0)

    plan("first")
    def between_first(step):
        plan("first%d" % step)
        if step == 0:
            make_bias()
            for k in range(1, NX):
                recv(bx.at[wrap(x - k, NX)], bx_ids[k])
        for k in A1.get(step, ()):
            att_heads(k, k + 1)

    gather(a0, a1, between_first, a1_ids)
    plan("out")
    w_done("out")

    whole = ow[...].reshape(D, HD)
    proj = []
    for buf, first, wide in ((a0, 0, C0), (a1, 2 * C0, C1)):
        pair = [whole[first + i * wide : first + (i + 1) * wide] for i in range(2)]
        pair = jnp.concatenate(pair, axis=1)
        proj.append(jnp.dot(buf[...].reshape(-1, wide), pair, preferred_element_type=F32))
    for col in range(NX * NZ):
        bx_, bz_ = block_of(col)
        r0, r1 = (bx_ * NZ + bz_) * 16, (bz_ * NX + bx_) * 16
        state[col * LAB : (col + 1) * LAB] = (
            bx[bx_, bz_, 0:LAB]
            + (proj[0][r0 : r0 + 8, :HD] + proj[0][r0 + 8 : r0 + 16, HD:])
            + (proj[1][r1 : r1 + 8, :HD] + proj[1][r1 + 8 : r1 + 16, HD:])
        )

    gain = gain_ref[...].astype(F32)
    sixteen = lax.broadcasted_iota(jnp.int32, (16, HD), 0)
    scaled = (state[...] * gain).astype(BF16)
    s1[z, x] = scaled[R0:]
    s0[x, z, 0:R0] = scaled[:R0]
    sums = jnp.zeros((16, HD), F32)
    for h in range(2):
        part = state[h * 128 : (h + 1) * 128]
        square = jnp.sum(jnp.transpose(part * part), axis=0, keepdims=True)
        top = square.astype(BF16).astype(F32)
        mid = (square - top).astype(BF16).astype(F32)
        for i, value in enumerate((top, mid, square - top - mid)):
            sums = jnp.where(sixteen == 3 * h + i, value, sums)
    s0[x, z, R0:] = sums.astype(BF16)

    plan("second")

    def between_second(step):
        plan("second%d" % step)
        for k in A2.get(step, ()):
            att_heads(k, k + 1)

    gather(s0, s1, between_second)
    plan("gu")
    w_done("gu")

    total = jnp.zeros((16, HD), F32)
    for i in range(NX):
        for j in range(NZ):
            total = total + s0[i, j, R0:].astype(F32)
    scale = []
    for h in range(2):
        line = jnp.sum(total[3 * h : 3 * h + 3], axis=0, keepdims=True)
        scale.append(lax.rsqrt(jnp.transpose(jnp.broadcast_to(line, (128, 128))) / D + 1e-5))
    scale = jnp.concatenate(scale, axis=0)
    acc[...] = jnp.zeros_like(acc)
    for c in range(2 * NY):
        pieces = []
        for col in range(4 * c, 4 * c + 4):
            bx_, bz_ = block_of(col)
            pieces.append(jnp.concatenate([s0[bx_, bz_, 0:R0], s1[bz_, bx_]], axis=0))
        acc[...] += nt(jnp.concatenate(pieces, axis=1), gu[c])
    scale = jnp.concatenate([scale] * 4, axis=1)[:, :FFL]
    gate = acc[:, :FFL] * scale
    up = acc[:, FFL:] * scale
    hidden = (gate / (1.0 + jnp.exp(-gate)) * up).astype(BF16)

    plan("down")
    w_done("down")
    own_reward = jnp.broadcast_to(rw_ref[...], (16, HD))
    high = state[...].astype(BF16)
    part_reward = nt(own_reward, high) + nt(own_reward, (state[...] - high.astype(F32)).astype(BF16))
    for c in range(2 * NY):
        terms = jnp.dot(hidden, dn[c], preferred_element_type=F32).astype(BF16)
        line = [bx[block_of(4 * c + i) + (slice(LAB, None),)] for i in range(4)]
        line = jnp.concatenate(line, axis=1)
        part_reward = part_reward + nt(jnp.concatenate([line, line], axis=0).astype(BF16), terms)
        for i in range(4):
            bx_, bz_ = block_of(4 * c + i)
            cols = terms[:, i * HD : (i + 1) * HD]
            tb0[bx_, bz_] = cols[:R0]
            tb1[bz_, bx_] = cols[R0:]

    lo, hi = pl.ds(0, NX // 2), pl.ds(NX // 2, NX // 2)
    chains = {
        "up_lo": (1, lo, 4, rp, sp),
        "dn_hi": (-1, hi, 4, rm, sm),
        "up_hi": (1, hi, 3, rp, sp),
        "dn_lo": (-1, lo, 3, rm, sm),
    }
    hop = {}
    for name, (k, part, count, got, _) in chains.items():
        hop[name] = send(tb1.at[wrap(z + k * count, NZ), part], got.at[0, part], "z", k)
    x_ids = {}
    order = (4, 3, -3, 2, -2, 1, -1, 0)

    def send_x(d):
        there = wrap(z + d, NZ)
        for k in (1, 3, 2):
            x_ids[d, k] = send(tb0.at[wrap(x + k, NX), there], rx0.at[x, there], "x", k)

    for d in order[:AHEAD]:
        send_x(d)
    prx[x] = part_reward[0:8]
    rx_ids = {k: send(prx.at[x], prx.at[x], "x", k) for k in range(1, NX)}
    for k in A3.get("start", ()):
        att_heads(k, k + 1)
    z_ids = {}

    def add_x(d):
        there = wrap(z + d, NZ)
        total = tb0[x, there].astype(F32)
        for k in (1, 3, 2):
            src = wrap(x - k, NX)
            recv(rx0.at[src, there], x_ids[d, k])
            total = total + rx0[src, there].astype(F32)
        if d in order[:-AHEAD]:
            send_x(order[order.index(d) + AHEAD])
        return total

    def pass_on(d):
        there = wrap(z + d, NZ)
        sb0[there] = add_x(d).astype(BF16)
        z_ids[d % NZ] = send(sb0.at[there], rz0.at[z], "z", d)

    for step in range(3):
        for name, (k, part, count, got, out) in chains.items():
            if step + 1 < count:
                recv(got.at[step, part], hop[name])
                own = tb1[wrap(z + k * (count - 1 - step), NZ), part]
                out[step, part] = (got[step, part].astype(F32) + own.astype(F32)).astype(BF16)
                hop[name] = send(out.at[step, part], got.at[step + 1, part], "z", k)
        for d in ((4, 3), (-3, 2), (-2, 1))[step]:
            pass_on(d)
    pass_on(-1)
    for k in range(1, NX):
        recv(prx.at[wrap(x - k, NX)], rx_ids[k])
    prz[z] = (prx[0] + prx[1]) + (prx[2] + prx[3])
    rz_ids = {k: send(prz.at[z], prz.at[z], "z", k) for k in range(1, NZ)}
    for name, (k, part, count, got, _) in chains.items():
        recv(got.at[count - 1, part], hop[name])
    for part, last_up, last_down in ((lo, 3, 2), (hi, 2, 3)):
        pair = rp[last_up, part].astype(F32) + rm[last_down, part].astype(F32)
        sb1[part] = (tb1[z, part].astype(F32) + pair).astype(BF16)
    far_ids = {k: send(sb1.at[wrap(x + k, NX)], rx1.at[x], "x", k) for k in range(1, NX)}
    for k in A3.get("end", ()):
        att_heads(k, k + 1)
    branch1 = sb1[x].astype(F32)
    for k in range(1, NX):
        src = wrap(x - k, NX)
        recv(rx1.at[src], far_ids[k])
        branch1 = branch1 + rx1[src].astype(F32)
    branch0 = add_x(0)
    for k in range(1, NZ):
        src = wrap(z - k, NZ)
        recv(rz0.at[src], z_ids[k])
        branch0 = branch0 + rz0[src].astype(F32)
    labeled = (state[...] + jnp.concatenate([branch0, branch1], axis=0)).astype(BF16)
    labeled_ref[...] = labeled
    for k in range(1, NZ):
        recv(prz.at[wrap(z - k, NZ)], rz_ids[k])
    total = prz[0]
    for i in range(1, NZ):
        total = total + prz[i]
    reward_ref[...] = total[0:1]

    for copy, cond in sent:
        if cond is None:
            copy.wait_send()
        else:
            pl.when(cond)(copy.wait_send)


def per_device(
    queries,
    keys,
    values,
    documents,
    residual,
    labels,
    out_weight,
    norm_gain,
    gate_weight,
    up_weight,
    down_weight,
    reward_weight,
):
    vmem = pl.BlockSpec(memory_space=pltpu.VMEM)
    hbm = pl.BlockSpec(memory_space=pl.ANY)
    smem = pl.BlockSpec(memory_space=pltpu.SMEM)
    attended, labeled, reward = pl.pallas_call(
        body,
        out_shape=(
            jax.ShapeDtypeStruct((1, TOK, D), BF16),
            jax.ShapeDtypeStruct((ROWS, HD), BF16),
            jax.ShapeDtypeStruct((1, ROWS), F32),
        ),
        in_specs=[hbm, hbm, hbm, vmem, hbm, smem, hbm, vmem, hbm, hbm, hbm, vmem],
        out_specs=(vmem, vmem, vmem),
        scratch_shapes=[
            pltpu.VMEM((1, TOK, D), BF16),
            pltpu.VMEM((1, TOK, D), BF16),
            pltpu.VMEM((8, TOK, KVH * HD), BF16),
            pltpu.VMEM((8, TOK, KVH * HD), BF16),
            pltpu.VMEM((8, 8, TOK), jnp.int32),
            pltpu.VMEM((8, 512, HD), BF16),
            pltpu.VMEM((8, 2 * FFL, 512), BF16),
            pltpu.VMEM((8, FFL, 512), BF16),
            pltpu.VMEM((TOK, 8 * TOK), F32),
            pltpu.VMEM((KVH, 4 * LAB, HD), BF16),
            pltpu.VMEM((KVH, 4 * LAB, HD), F32),
            pltpu.VMEM((NX, NZ, 16, C0), BF16),
            pltpu.VMEM((NZ, NX, 16, C1), BF16),
            pltpu.VMEM((NZ, NX, 2 * LAB, HD), F32),
            pltpu.VMEM((NZ, NX, 2 * LAB, HD), F32),
            pltpu.VMEM((NX, NZ, 2 * LAB, HD), F32),
            pltpu.VMEM((ROWS, HD), F32),
            pltpu.VMEM((NX, NZ, R0 + 16, HD), BF16),
            pltpu.VMEM((NZ, NX, R1, HD), BF16),
            pltpu.VMEM((ROWS, 2 * FFL), F32),
            pltpu.VMEM((NX, NZ, R0, HD), BF16),
            pltpu.VMEM((NX, NZ, R0, HD), BF16),
            pltpu.VMEM((NZ, R0, HD), BF16),
            pltpu.VMEM((NZ, R0, HD), BF16),
            pltpu.VMEM((NZ, NX, R1, HD), BF16),
            pltpu.VMEM((4, NX, R1, HD), BF16),
            pltpu.VMEM((4, NX, R1, HD), BF16),
            pltpu.VMEM((3, NX, R1, HD), BF16),
            pltpu.VMEM((3, NX, R1, HD), BF16),
            pltpu.VMEM((NX, R1, HD), BF16),
            pltpu.VMEM((NX, R1, HD), BF16),
            pltpu.VMEM((NX, 8, ROWS), F32),
            pltpu.VMEM((NZ, 8, ROWS), F32),
            pltpu.SemaphoreType.DMA((NSEM,)),
            pltpu.SemaphoreType.DMA((NSEM,)),
            pltpu.SemaphoreType.DMA((8,)),
        ],
        compiler_params=pltpu.CompilerParams(
            collective_id=0, has_side_effects=True, vmem_limit_bytes=56 * 1024 * 1024
        ),
        name="layer",
    )(
        queries,
        keys,
        values,
        documents,
        residual,
        labels,
        out_weight,
        norm_gain.reshape(1, HD),
        gate_weight.T,
        up_weight.T,
        down_weight,
        reward_weight.reshape(1, HD),
    )
    return attended, labeled, reward.reshape(ROWS)


def solution(mesh):
    return jax.shard_map(
        per_device,
        mesh=mesh,
        in_specs=(
            P(("grp", "tp"), "ctx", None),
            P(("grp", "tp"), "ctx", None),
            P(("grp", "tp"), "ctx", None),
            P(("grp", "tp"), "ctx"),
            P(("grp", "tp"), "ctx", None),
            P(("grp", "tp"), "ctx"),
            P("ctx", ("grp", "tp")),
            P(("grp", "tp")),
            P("ctx", ("grp", "tp")),
            P("ctx", ("grp", "tp")),
            P(("grp", "tp"), "ctx"),
            P(("grp", "tp")),
        ),
        out_specs=(P(("grp", "tp"), "ctx", None), P("ctx", ("grp", "tp")), P("ctx")),
        check_vma=False,
    )
```
